256 devices in a mesh: facet: 16 (over x, y_lo, core), freq: 16 (over z, y_hi).
Axes of the slice: x: 4, y: 4 (y_hi: 2, y_lo: 2; y = y_hi * 2 + y_lo), z: 8, core: 2. Of those that a mesh axis runs over, the one named last changes fastest.
Arguments:
- residual: float32 [32, 16, 512, 512], P('freq', 'facet'), may hold values from -3 to 3
- components: bfloat16 [4, 32, 128, 128], P(None, 'freq', 'facet'), may hold values from -6 to 6
- chan_weight: float32 [32], P('freq'), may hold values from 0.3 to 3
- tile_pos: int32 [4, 2], replicated, may hold values from 0 to 1920, as said below
- facet_psf: int32 [16], P('facet'), may hold values from 0 to 3
- psf_spectra: bfloat16 [4, 32, 2, 768, 768], P(None, 'freq', None, 'facet'), may hold values from -48 to 48
Outputs:
- new_residual: float32 [32, 16, 512, 512], P('freq', 'facet')
The draws below stay inside these ranges and needn't reach their ends.
Inputs may be any that keep to these rules, and one draw needn't show every extreme that they name: `tile_pos`: each row is a tile's top-left pixel (row, column); the row never exceeds 2048 - 128 and the column never exceeds 2048 - 128; some tile lies at the image's right edge and some tile at its top edge.
All inputs are finite; a program needn't handle non-finite values.
Results may differ from the reference program's by a relative error of at most 0.0045.
Values may be sent and summed in bfloat16 or wider, within the bound.
A program may use at most 128 MiB of HBM per device.

```python
import math
import jax
import jax.numpy as jnp
from jax import lax

CHAN = 32
FS = 512
PAD = 128
TS = 128
NTILE = 4
FCOLS = 4
NPSF = 4
FRAME = 768
FACETS = 16
IMG_ROWS = 2048
IMG_COLS = 2048


def draw_tile_pos(key, part):
    key_center, key_offset = jax.random.split(jax.random.fold_in(key, 11))
    center = jax.random.randint(key_center, (), 0, FACETS)
    middle_row = center // FCOLS * FS + FS // 2 - TS // 2
    middle_col = center % FCOLS * FS + FS // 2 - TS // 2
    shifts = jax.random.randint(key_offset, (NTILE, 2), -FS, FS + 1)
    tile_rows = jnp.clip(middle_row + shifts[:, 0], 0, IMG_ROWS - TS)
    tile_cols = jnp.clip(middle_col + shifts[:, 1], 0, IMG_COLS - TS)
    tile_index = jnp.arange(NTILE, dtype=jnp.int32)
    tile_cols = jnp.where(tile_index == 0, IMG_COLS - TS, tile_cols)
    tile_rows = jnp.where(tile_index == 1, 0, tile_rows)
    return jnp.stack([tile_rows, tile_cols], axis=1).astype(jnp.int32)


def touch_ends(values, stream_key, least, high):
    extent = values.shape
    place = [jax.random.randint(jax.random.fold_in(stream_key, axis), (), 0, extent[axis]) for axis in range(len(extent))]
    values = values.at[tuple(place)].set(least)
    longest = extent.index(max(extent))
    place[longest] = (place[longest] + 1) % extent[longest]
    return values.at[tuple(place)].set(high)


def block_levels(own_key, extent, cuts, smallest, top_value):
    factor_of = 1.0
    for axis_at, parts in cuts:
        draws = jax.random.uniform(jax.random.fold_in(jax.random.fold_in(own_key, 6), axis_at), (parts,), jnp.float32, smallest / len(cuts), top_value / len(cuts))
        factor_of = factor_of * jnp.repeat(jnp.exp(draws), extent[axis_at] // parts).reshape((-1,) + (1,) * (len(extent) - 1 - axis_at))
    return factor_of


def noise(stream_key, extent, width, reach, shards=(), kind=jnp.bfloat16):
    level = block_levels(stream_key, extent, shards, -0.22, 0.18) if shards else 1.0
    values = jax.random.normal(stream_key, extent, jnp.float32) * width * level
    return jnp.minimum(jnp.maximum(values, -reach), reach).astype(kind)


def setup_inputs(seed: int = 0) -> dict:
    key_of = jax.random.split(jax.random.key(seed), 7)
    residual = noise(key_of[0], (CHAN, FACETS, FS, FS), 0.5, 3.0, ((0, 16), (1, 16)), jnp.float32)
    components = noise(key_of[1], (NTILE, CHAN, TS, TS), 1.0, 6.0, ((1, 16), (2, 16)))
    chan_weight = jnp.clip(jnp.exp(math.log(3.0) - 2.3025851 * jax.random.uniform(key_of[2], (CHAN,), jnp.float32) ** block_levels(key_of[2], (CHAN,), ((0, 16),), -0.2, 0.2)), 0.3, 3.0)
    tile_pos = draw_tile_pos(jax.random.fold_in(key_of[6], 71), 0)
    facet_psf = touch_ends(jax.random.randint(key_of[4], (FACETS,), 0, NPSF), jax.random.fold_in(key_of[4], 1), 0, NPSF - 1).astype(jnp.int32)
    psf_spectra = noise(key_of[5], (NPSF, CHAN, 2, FRAME, FRAME), 8.0, 48.0, ((1, 16), (3, 16)))
    return {"residual": residual, "components": components, "chan_weight": chan_weight, "tile_pos": tile_pos, "facet_psf": facet_psf, "psf_spectra": psf_spectra}


def phase_table(positions):
    frequencies = jnp.arange(FRAME, dtype=jnp.int32)
    product = (positions[..., None] * frequencies) % FRAME
    theta = product.astype(jnp.float32) * (2.0 * math.pi / FRAME)
    return jnp.cos(theta), jnp.sin(theta)


def solve_fit(moments, gram_terms):
    g0, g1, g2, g3, g4 = gram_terms[0], gram_terms[1], gram_terms[2], gram_terms[3], gram_terms[4]
    c00 = g2 * g4 - g3 * g3
    c01 = g2 * g3 - g1 * g4
    c02 = g1 * g3 - g2 * g2
    c11 = g0 * g4 - g2 * g2
    c12 = g1 * g2 - g0 * g3
    c22 = g0 * g2 - g1 * g1
    determinant = g0 * c00 + g1 * c01 + g2 * c02
    first = (c00 * moments[0] + c01 * moments[1] + c02 * moments[2]) / determinant
    second = (c01 * moments[0] + c11 * moments[1] + c12 * moments[2]) / determinant
    third = (c02 * moments[0] + c12 * moments[1] + c22 * moments[2]) / determinant
    return jnp.stack([first, second, third])


def reference(residual, components, chan_weight, tile_pos, facet_psf, psf_spectra):
    channel = jnp.arange(CHAN, dtype=jnp.int32).astype(jnp.float32)
    freqs = (2.0 * channel - (CHAN - 1)) / CHAN
    comp_full = components.astype(jnp.float32)
    powers = [chan_weight, chan_weight * freqs, chan_weight * freqs * freqs]
    moments = jnp.stack([jnp.einsum('c,tcrs->trs', power, comp_full, precision=lax.Precision.HIGHEST) for power in powers])
    gram_terms = jnp.stack([jnp.sum(powers[0]), jnp.sum(powers[1]), jnp.sum(powers[2]),
                            jnp.sum(powers[2] * freqs), jnp.sum(powers[2] * freqs * freqs)])
    coefficients = solve_fit(moments, gram_terms).astype(jnp.bfloat16).astype(jnp.float32)
    model = (coefficients[0][:, None] + coefficients[1][:, None] * freqs[None, :, None, None]
             + coefficients[2][:, None] * (freqs * freqs)[None, :, None, None]).astype(jnp.bfloat16).astype(jnp.float32)
    inv_cos, inv_sin = phase_table(PAD + jnp.arange(FS, dtype=jnp.int32))
    inv_re = inv_cos.astype(jnp.bfloat16).astype(jnp.float32)
    inv_im = inv_sin.astype(jnp.bfloat16).astype(jnp.float32)
    local_pixels = jnp.arange(TS, dtype=jnp.int32)
    high = lax.Precision.HIGHEST

    def one_facet(facet):
        offset_rows = tile_pos[:, 0] - (facet // FCOLS) * FS + PAD
        offset_cols = tile_pos[:, 1] - (facet % FCOLS) * FS + PAD
        inside = ((offset_rows >= 0) & (offset_rows <= FRAME - TS) & (offset_cols >= 0)
                  & (offset_cols <= FRAME - TS)).astype(jnp.float32)[:, None, None]
        col_cos, col_sin = phase_table(offset_cols[:, None] + local_pixels[None, :])
        col_re = col_cos.astype(jnp.bfloat16).astype(jnp.float32)
        col_im = (-col_sin).astype(jnp.bfloat16).astype(jnp.float32)
        row_cos, row_sin = phase_table(offset_rows[:, None] + local_pixels[None, :])
        row_re = (row_cos * inside).astype(jnp.bfloat16).astype(jnp.float32)
        row_im = (-row_sin * inside).astype(jnp.bfloat16).astype(jnp.float32)
        u_re = jnp.einsum('tcrs,tsl->tcrl', model, col_re, precision=high).astype(jnp.bfloat16).astype(jnp.float32)
        u_im = jnp.einsum('tcrs,tsl->tcrl', model, col_im, precision=high).astype(jnp.bfloat16).astype(jnp.float32)
        spec_re = (jnp.einsum('trk,tcrl->ckl', row_re, u_re, precision=high)
                   - jnp.einsum('trk,tcrl->ckl', row_im, u_im, precision=high))
        spec_im = (jnp.einsum('trk,tcrl->ckl', row_re, u_im, precision=high)
                   + jnp.einsum('trk,tcrl->ckl', row_im, u_re, precision=high))
        chosen = psf_spectra[facet_psf[facet]].astype(jnp.float32)
        prod_re = (spec_re * chosen[:, 0] - spec_im * chosen[:, 1]).astype(jnp.bfloat16).astype(jnp.float32)
        prod_im = (spec_re * chosen[:, 1] + spec_im * chosen[:, 0]).astype(jnp.bfloat16).astype(jnp.float32)
        v_re = (jnp.einsum('yk,ckl->cyl', inv_re, prod_re, precision=high)
                - jnp.einsum('yk,ckl->cyl', inv_im, prod_im, precision=high)).astype(jnp.bfloat16).astype(jnp.float32)
        v_im = (jnp.einsum('yk,ckl->cyl', inv_re, prod_im, precision=high)
                + jnp.einsum('yk,ckl->cyl', inv_im, prod_re, precision=high)).astype(jnp.bfloat16).astype(jnp.float32)
        convolved = (jnp.einsum('cyl,xl->cyx', v_re, inv_re, precision=high)
                     - jnp.einsum('cyl,xl->cyx', v_im, inv_im, precision=high)) / (FRAME * FRAME)
        return residual[:, facet] - convolved

    result = lax.map(one_facet, jnp.arange(FACETS, dtype=jnp.int32))
    return jnp.transpose(result, (1, 0, 2, 3))
```

```python
import functools
import math

import jax
import jax.numpy as jnp
import ml_dtypes
import numpy as np
from jax import lax
from jax.experimental import pallas as pl
from jax.experimental.pallas import tpu as pltpu
from jax.sharding import PartitionSpec as P

CHAN = 32
FS = 512
PAD = 128
TS = 128
NTILE = 4
FCOLS = 4
FRAME = 768
N = 16
ROWS = 48
SLOTS = 24
MIB = 1 << 20
MESH = pl.DeviceIdType.MESH
VMEM = pl.BlockSpec(memory_space=pltpu.VMEM)
SMEM = pl.BlockSpec(memory_space=pltpu.SMEM)
f32 = jnp.float32
bf16 = jnp.bfloat16


def own_row(m, slot):
    return 0 if slot == 0 and m >= N // 2 else SLOTS + slot


def angles(left, right):
    return (left * right % FRAME).astype(np.float64) * (2.0 * math.pi / FRAME)


def half(table):
    return table.astype(ml_dtypes.bfloat16)


@functools.cache
def tables():
    slot_of = np.arange(4)[:, None, None] * 8 + np.arange(8)[None, None, :]
    slot_of = np.broadcast_to(slot_of, (4, 2, 8)).reshape(-1)
    chan_of = np.broadcast_to(np.arange(2)[None, :, None], (4, 2, 8)).reshape(-1)
    k_rows = np.zeros((N, 64), np.int64)
    own = np.zeros((N, 48, 96))
    mirror = np.zeros((48, 96))
    for m in range(N):
        for r in range(48):
            k_rows[m, r] = ROWS * m + own_row(m, slot_of[r])
            own[m, r, chan_of[r] * ROWS + own_row(m, slot_of[r])] = 1.0
    for r in range(48):
        mirror[r, chan_of[r] * ROWS + SLOTS - slot_of[r]] = 1.0
    tile_rows = np.arange(N)[:, None, None] * 8 + np.arange(8)[None, None, :]
    tile_rows = np.broadcast_to(tile_rows, (N, 2, 8)).reshape(-1)
    tile_chan = np.broadcast_to(np.arange(2)[None, :, None], (N, 2, 8)).reshape(-1)
    theta = angles(k_rows[:, :, None], tile_rows[None, None, :])
    same = (chan_of[:, None] == tile_chan[None, :])[None]
    rows = np.concatenate([np.cos(theta) * same, -np.sin(theta) * same], axis=1)
    theta = angles(np.arange(TS)[:, None], np.arange(FRAME)[None, :])
    cos, sin = np.cos(theta), np.sin(theta)
    cols = np.block([[cos, -sin], [sin, cos]])
    theta = angles(np.arange(FRAME)[:, None], PAD + np.arange(FS)[None, :])
    cos, sin = np.cos(theta), np.sin(theta)
    back_cols = np.block([[cos, sin], [-sin, cos]])
    back_rows = np.zeros((FS, N, 2, SLOTS))
    y = PAD + np.arange(FS)
    for m in range(N):
        for slot in range(SLOTS):
            theta = angles(np.int64(ROWS * m + own_row(m, slot)), y)
            back_rows[:, m, 0, slot] = np.cos(theta)
            back_rows[:, m, 1, slot] = -np.sin(theta)
    back_rows[:, N // 2, 0, 0] *= 0.5
    back_rows[:, N // 2, 1, 0] = 0.5
    flip = np.zeros((FRAME, FRAME))
    flip[(FRAME - np.arange(FRAME)) % FRAME, np.arange(FRAME)] = 1.0
    return dict(
        k_rows=k_rows.astype(np.int32),
        own=half(own),
        mirror=half(mirror),
        rows=half(rows),
        cols=half(cols),
        back_cols=half(back_cols),
        back_rows=half(back_rows.reshape(FS, N * 2 * SLOTS)),
        flip=half(flip),
    )


def channel_at(index):
    return (2 * index - (CHAN - 1)).astype(f32) * (1.0 / CHAN)


def exchange_kernel(
    comps_ref, weight_ref, psf_of_ref, psf_ref, row0_ref, mirror_ref,
    model_ref, far_ref, far0_ref,
    send_a, recv_a, send_b, send_m,
    a_send, a_recv, b_send, b_recv, m_send, m_recv,
):
    facet = lax.axis_index("facet")
    freq = lax.axis_index("freq")
    barrier = pltpu.get_barrier_semaphore()

    def greet(d, _):
        pl.semaphore_signal(barrier, inc=1, device_id={"freq": (freq + d) % N}, device_id_type=MESH)
        pl.semaphore_signal(barrier, inc=1, device_id={"facet": (facet + d) % N}, device_id_type=MESH)
        return 0

    lax.fori_loop(1, N, greet, 0)

    send_a[0:64, :] = comps_ref[...]
    row = lax.broadcasted_iota(jnp.int32, (8, 128), 0)
    parts = []
    for c in range(2):
        whole = jnp.full((8, 128), weight_ref[c], f32)
        first = whole.astype(bf16).astype(f32)
        second = (whole - first).astype(bf16).astype(f32)
        third = (whole - first) - second
        parts.append(jnp.where(row == 0, first, jnp.where(row == 1, second, jnp.where(row == 2, third, 0.0))))
    send_a[64:80, :] = jnp.concatenate(parts, axis=0).astype(bf16)
    pl.semaphore_wait(barrier, 2 * (N - 1))

    def copy_a(d, slot):
        return pltpu.make_async_remote_copy(
            src_ref=send_a, dst_ref=recv_a.at[slot], send_sem=a_send.at[d], recv_sem=a_recv.at[slot],
            device_id={"freq": (freq + d) % N}, device_id_type=MESH,
        )

    def copy_b(d, slot):
        return pltpu.make_async_remote_copy(
            src_ref=send_b, dst_ref=model_ref.at[slot], send_sem=b_send.at[d], recv_sem=b_recv.at[slot],
            device_id={"facet": (facet + d) % N}, device_id_type=MESH,
        )

    def start_a(d, _):
        copy_a(d, freq).start()
        return 0

    lax.fori_loop(1, N, start_a, 0)
    recv_a[freq] = send_a[...]

    for index in range(8):
        both = psf_ref[index // 2, :, index % 2].reshape(2 * ROWS, FRAME)
        send_m[index] = jnp.dot(mirror_ref[...], both, preferred_element_type=f32).astype(bf16)
    copy_m = pltpu.make_async_remote_copy(
        src_ref=send_m, dst_ref=far_ref, send_sem=m_send.at[0], recv_sem=m_recv.at[0],
        device_id={"facet": N - 1 - facet}, device_id_type=MESH,
    )
    copy_m.start()
    is_first = 1 - (facet + N - 1) // N
    is_middle = 1 - ((facet + N // 2) % N + N - 1) // N
    copy_0 = pltpu.make_async_remote_copy(
        src_ref=row0_ref, dst_ref=far0_ref, send_sem=m_send.at[1], recv_sem=m_recv.at[1],
        device_id={"facet": (N - facet) % N + (N // 2) * (is_first - is_middle)}, device_id_type=MESH,
    )
    copy_0.start()

    def land_a(d, _):
        copy_a(d, (freq + N - d) % N).wait_recv()
        return 0

    lax.fori_loop(1, N, land_a, 0)

    def add(q, total):
        total = list(total)
        block = recv_a[q].astype(f32)
        comp = block[0:64].reshape(NTILE, 2, 8, 128)
        for c in range(2):
            x = channel_at(2 * q + c)
            power = jnp.sum(block[64 + 8 * c : 72 + 8 * c], axis=0, keepdims=True)
            for j in range(5):
                if j < 3:
                    total[j] = total[j] + power * comp[:, c]
                total[3 + j] = total[3 + j] + power
                power = power * x
        return tuple(total)

    zeros = tuple(jnp.zeros((NTILE, 8, 128), f32) for _ in range(3)) + tuple(jnp.zeros((1, 128), f32) for _ in range(5))
    m0, m1, m2, g0, g1, g2, g3, g4 = lax.fori_loop(0, N, add, zeros)
    c00 = g2 * g4 - g3 * g3
    c01 = g2 * g3 - g1 * g4
    c02 = g1 * g3 - g2 * g2
    c11 = g0 * g4 - g2 * g2
    c12 = g1 * g2 - g0 * g3
    c22 = g0 * g2 - g1 * g1
    det = g0 * c00 + g1 * c01 + g2 * c02
    a0 = ((c00 * m0 + c01 * m1 + c02 * m2) / det).astype(bf16).astype(f32)
    a1 = ((c01 * m0 + c11 * m1 + c12 * m2) / det).astype(bf16).astype(f32)
    a2 = ((c02 * m0 + c12 * m1 + c22 * m2) / det).astype(bf16).astype(f32)
    both = []
    for c in range(2):
        x = channel_at(2 * freq + c)
        both.append(a0 + a1 * x + a2 * (x * x))
    send_b[0:64, :] = jnp.stack(both, axis=1).reshape(64, 128).astype(bf16)
    send_b[64:80, :] = jnp.full((16, 128), psf_of_ref[0].astype(f32), f32).astype(bf16)

    def start_b(d, _):
        copy_b(d, facet).start()
        return 0

    lax.fori_loop(1, N, start_b, 0)
    model_ref[facet] = send_b[...]

    def land_b(d, _):
        copy_b(d, (facet + N - d) % N).wait_recv()
        copy_a(d, freq).wait_send()
        copy_b(d, facet).wait_send()
        return 0

    lax.fori_loop(1, N, land_b, 0)
    copy_0.wait()
    copy_m.wait()


def exchange(comps, weight, psf_of, psf, row0, mirror):
    dma = pltpu.SemaphoreType.DMA
    return pl.pallas_call(
        exchange_kernel,
        out_shape=(
            jax.ShapeDtypeStruct((N, 80, 128), bf16),
            jax.ShapeDtypeStruct((8, 48, FRAME), bf16),
            jax.ShapeDtypeStruct((16, FRAME), bf16),
        ),
        in_specs=[VMEM, SMEM, SMEM, VMEM, VMEM, VMEM],
        out_specs=(VMEM, VMEM, VMEM),
        scratch_shapes=[
            pltpu.VMEM((80, 128), bf16),
            pltpu.VMEM((N, 80, 128), bf16),
            pltpu.VMEM((80, 128), bf16),
            pltpu.VMEM((8, 48, FRAME), bf16),
            dma((N,)), dma((N,)), dma((N,)), dma((N,)), dma((2,)), dma((2,)),
        ],
        compiler_params=pltpu.CompilerParams(collective_id=0, has_side_effects=True, vmem_limit_bytes=24 * MIB),
        name="exchange",
    )(comps, weight, psf_of, psf, row0, mirror)


def product_kernel(
    tile_pos_ref, model_ref, psf_ref, far_ref, far0_ref, own_ref, flip_ref, rows_ref, cols_ref, row_ph_ref, col_ph_ref,
    out_ref,
    psf_sum, back, tiles, spec,
):
    facet = lax.axis_index("facet")
    middle = facet == N // 2
    upper = facet >= N // 2

    for t in range(NTILE):
        model = model_ref[:, 16 * t : 16 * t + 16, :].reshape(256, 128)
        half_way = jnp.dot(rows_ref[...], model, preferred_element_type=f32).astype(bf16)
        half_way = jnp.concatenate([half_way[0:64], half_way[64:128]], axis=1)
        tiles[t] = jnp.dot(half_way, cols_ref[...], preferred_element_type=f32)

    row = lax.broadcasted_iota(jnp.int32, (16, FRAME), 0)
    for index in range(8):
        p, ri = index // 2, index % 2
        both = psf_ref[p, :, ri].reshape(2 * ROWS, FRAME)
        chosen = jnp.dot(own_ref[...], both, preferred_element_type=f32)
        psf_sum[p, ri, 0:48] = chosen
        zero_row = [far0_ref[4 * p + 2 * c + ri : 4 * p + 2 * c + ri + 1].astype(f32) for c in range(2)]
        zero_rows = jnp.where(row == 0, zero_row[0], jnp.where(row == 8, zero_row[1], 0.0))
        psf_sum[p, ri, 48:64] = zero_rows
        far = far_ref[index].astype(f32)
        lead = jnp.where((row % 8 == 0) & upper, jnp.where(middle, chosen[0:16], zero_rows), far[0:16])
        back[index, 0:16] = lead.astype(bf16)
        back[index, 16:48] = far_ref[index, 16:48]
        back[index, 48:64] = zero_rows.astype(bf16)
    for index in range(8):
        p, ri = index // 2, index % 2
        flipped = jnp.dot(back[index], flip_ref[...], preferred_element_type=f32)
        psf_sum[p, ri] = psf_sum[p, ri] + (flipped if ri == 0 else -flipped)

    lane = lax.broadcasted_iota(jnp.int32, (64, 128), 1)

    def one_facet(f, _):
        a, b = f // FCOLS, f % FCOLS
        counted = []
        for t in range(NTILE):
            oy = tile_pos_ref[t, 0] - a * FS + PAD
            ox = tile_pos_ref[t, 1] - b * FS + PAD
            counted.append((oy >= 0) & (oy <= FRAME - TS) & (ox >= 0) & (ox <= FRAME - TS))
        some = counted[0] | counted[1] | counted[2] | counted[3]

        @pl.when(jnp.logical_not(some))
        def _():
            out_ref[f] = jnp.zeros((48, 2 * FRAME), bf16)

        @pl.when(some)
        def _():
            spec[...] = jnp.zeros_like(spec)
            for t in range(NTILE):

                @pl.when(counted[t])
                def _():
                    at = t * FCOLS + a
                    rc = jnp.sum(jnp.where(lane == at, row_ph_ref[...], 0.0), axis=1, keepdims=True)
                    rs = jnp.sum(jnp.where(lane == at + 16, row_ph_ref[...], 0.0), axis=1, keepdims=True)
                    cc = col_ph_ref[0, pl.ds(t * FCOLS + b, 1), :]
                    cs = col_ph_ref[1, pl.ds(t * FCOLS + b, 1), :]

                    def group(g):
                        at = slice(16 * g, 16 * g + 16)
                        pr = rc[at] * cc - rs[at] * cs
                        pi = rc[at] * cs + rs[at] * cc
                        tr = tiles[t, at, 0:FRAME]
                        ti = tiles[t, at, FRAME : 2 * FRAME]
                        spec[0, at] = spec[0, at] + (pr * tr - pi * ti)
                        spec[1, at] = spec[1, at] + (pr * ti + pi * tr)

                    for g in range(3):
                        group(g)

                    @pl.when(middle)
                    def _():
                        group(3)

            psf = jnp.max(model_ref[f, 64:80, :].astype(f32)).astype(jnp.int32)

            def group(g):
                at = slice(16 * g, 16 * g + 16)
                sr, si = spec[0, at], spec[1, at]
                hr, hi = psf_sum[psf, 0, at], psf_sum[psf, 1, at]
                return sr * hr - si * hi, sr * hi + si * hr

            for g in range(3):
                re, im = group(g)
                out_ref[f, 16 * g : 16 * g + 16, 0:FRAME] = re.astype(bf16)
                out_ref[f, 16 * g : 16 * g + 16, FRAME : 2 * FRAME] = im.astype(bf16)

            @pl.when(middle)
            def _():
                re, im = group(0)
                more_re, more_im = group(3)
                out_ref[f, 0:16, 0:FRAME] = (re - more_im).astype(bf16)
                out_ref[f, 0:16, FRAME : 2 * FRAME] = (im + more_re).astype(bf16)

        return 0

    lax.fori_loop(0, N, one_facet, 0)


def products(*args):
    return pl.pallas_call(
        product_kernel,
        out_shape=jax.ShapeDtypeStruct((N, 48, 2 * FRAME), bf16),
        in_specs=[SMEM] + [VMEM] * 10,
        out_specs=VMEM,
        scratch_shapes=[
            pltpu.VMEM((4, 2, 64, FRAME), f32),
            pltpu.VMEM((8, 64, FRAME), bf16),
            pltpu.VMEM((NTILE, 64, 2 * FRAME), f32),
            pltpu.VMEM((2, 64, FRAME), f32),
        ],
        compiler_params=pltpu.CompilerParams(vmem_limit_bytes=24 * MIB),
        name="products",
    )(*args)


def columns_kernel(prod_ref, back_ref, out_ref, send, sent, landed):
    facet = lax.axis_index("facet")
    freq = lax.axis_index("freq")
    del freq
    barrier = pltpu.get_barrier_semaphore()

    def greet(d, _):
        pl.semaphore_signal(barrier, inc=1, device_id={"facet": (facet + d) % N}, device_id_type=MESH)
        return 0

    lax.fori_loop(1, N, greet, 0)

    def copy(to, slot):
        return pltpu.make_async_remote_copy(
            src_ref=send.at[to], dst_ref=out_ref.at[:, slot], send_sem=sent.at[to], recv_sem=landed.at[slot],
            device_id={"facet": to}, device_id_type=MESH,
        )

    mine = facet // FCOLS
    within = facet % FCOLS
    for step, shift in enumerate((2, 1, 3, 0)):
        a = (mine + shift) % FCOLS
        block = prod_ref[pl.ds(a * FCOLS, FCOLS)].reshape(FCOLS * 48, 2 * FRAME)
        w = jnp.dot(block, back_ref[...], preferred_element_type=f32)
        w = w.reshape(FCOLS, 3, 2, 8, 2 * FS)
        for b in range(FCOLS):
            for c in range(2):
                for ri in range(2):
                    part = w[b, :, c, :, ri * FS : (ri + 1) * FS].reshape(SLOTS, FS)
                    if ri == 0:
                        real = part
                send[a * FCOLS + b, c] = jnp.concatenate([real, part], axis=0).astype(bf16)
        if step == 0:
            pl.semaphore_wait(barrier, N - 1)
        for j in range(FCOLS):
            if shift == 0 and j == 0:
                continue
            copy(a * FCOLS + (within + j) % FCOLS, facet).start()
    for c in range(2):
        out_ref[c, facet] = send[facet, c]

    def land(d, _):
        copy((facet + N - d) % N, (facet + N - d) % N).wait()
        return 0

    lax.fori_loop(1, N, land, 0)


def columns(prod, back):
    dma = pltpu.SemaphoreType.DMA
    return pl.pallas_call(
        columns_kernel,
        out_shape=jax.ShapeDtypeStruct((2, N, 48, FS), bf16),
        in_specs=[VMEM, VMEM],
        out_specs=VMEM,
        scratch_shapes=[pltpu.VMEM((N, 2, 48, FS), bf16), dma((N,)), dma((N,))],
        compiler_params=pltpu.CompilerParams(collective_id=1, has_side_effects=True, vmem_limit_bytes=24 * MIB),
        name="columns",
    )(prod, back)


def rows_kernel(residual_ref, w_ref, back_ref, out_ref):
    convolved = jnp.dot(back_ref[...], w_ref[0], preferred_element_type=f32)
    out_ref[0, 0] = residual_ref[0, 0] - convolved * (1.0 / (FRAME * FRAME))


def subtract(residual, w, back):
    return pl.pallas_call(
        rows_kernel,
        grid=(2,),
        out_shape=jax.ShapeDtypeStruct(residual.shape, f32),
        in_specs=[
            pl.BlockSpec((1, 1, FS, FS), lambda c: (c, 0, 0, 0)),
            pl.BlockSpec((1, FRAME, FS), lambda c: (c, 0, 0)),
            pl.BlockSpec((FS, FRAME), lambda c: (0, 0)),
        ],
        out_specs=pl.BlockSpec((1, 1, FS, FS), lambda c: (c, 0, 0, 0)),
        compiler_params=pltpu.CompilerParams(vmem_limit_bytes=24 * MIB),
        name="subtract",
    )(residual, w, back)


def phases(products):
    theta = (products % FRAME).astype(f32) * (2.0 * math.pi / FRAME)
    return jnp.cos(theta), -jnp.sin(theta)


def shards(residual, components, chan_weight, tile_pos, facet_psf, psf_spectra):
    table = {name: jnp.asarray(value) for name, value in tables().items()}
    facet = lax.axis_index("facet")

    def mine(name):
        return lax.dynamic_index_in_dim(table[name], facet, 0, keepdims=False)

    anchors = jnp.arange(FCOLS, dtype=jnp.int32) * FS - PAD
    oy = (tile_pos[:, 0][:, None] - anchors).reshape(-1)
    ox = (tile_pos[:, 1][:, None] - anchors).reshape(-1)
    row_ph = jnp.concatenate(phases(mine("k_rows")[:, None] * oy[None, :]), axis=1)
    row_ph = jnp.pad(row_ph, ((0, 0), (0, 96)))
    col_ph = jnp.stack(phases(ox[:, None] * jnp.arange(FRAME, dtype=jnp.int32)[None, :]))
    model, far, far0 = exchange(
        components.reshape(64, 128), chan_weight, facet_psf, psf_spectra,
        psf_spectra[:, :, :, 0, :].reshape(16, FRAME), table["mirror"],
    )
    prod = products(
        tile_pos, model, psf_spectra, far, far0, mine("own"), table["flip"], mine("rows"), table["cols"], row_ph, col_ph,
    )
    w = columns(prod, table["back_cols"])
    return subtract(residual, w.reshape(2, FRAME, FS), table["back_rows"])


def solution(mesh):
    placed = (
        P("freq", "facet", None, None),
        P(None, "freq", "facet", None),
        P("freq"),
        P(),
        P("facet"),
        P(None, "freq", None, "facet", None),
    )
    return jax.shard_map(
        shards,
        mesh=mesh,
        in_specs=placed,
        out_specs=P("freq", "facet", None, None),
        check_vma=False,
    )
```

```python
import functools
import math

import jax
import jax.numpy as jnp
import ml_dtypes
import numpy as np
from jax import lax
from jax.experimental import pallas as pl
from jax.experimental.pallas import tpu as pltpu
from jax.sharding import PartitionSpec as P

CHAN = 32
FS = 512
PAD = 128
TS = 128
NTILE = 4
FCOLS = 4
FRAME = 768
N = 16
ROWS = 48
SLOTS = 24
MIB = 1 << 20
MESH = pl.DeviceIdType.MESH
VMEM = pl.BlockSpec(memory_space=pltpu.VMEM)
HBM = pl.BlockSpec(memory_space=pltpu.HBM)
f32 = jnp.float32
bf16 = jnp.bfloat16


def own_row(m, slot):
    return 0 if slot == 0 and m >= N // 2 else SLOTS + slot


def angles(left, right):
    return (left * right % FRAME).astype(np.float64) * (2.0 * math.pi / FRAME)


def half(table):
    return table.astype(ml_dtypes.bfloat16)


@functools.cache
def tables():
    slot_of = np.arange(4)[:, None, None] * 8 + np.arange(8)[None, None, :]
    slot_of = np.broadcast_to(slot_of, (4, 2, 8)).reshape(-1)
    chan_of = np.broadcast_to(np.arange(2)[None, :, None], (4, 2, 8)).reshape(-1)
    k_rows = np.zeros((N, 64), np.int64)
    own = np.zeros((N, 48, 96))
    mirror = np.zeros((48, 96))
    for m in range(N):
        for r in range(48):
            k_rows[m, r] = ROWS * m + own_row(m, slot_of[r])
            own[m, r, chan_of[r] * ROWS + own_row(m, slot_of[r])] = 1.0
    for r in range(48):
        mirror[r, chan_of[r] * ROWS + SLOTS - slot_of[r]] = 1.0
    tile_rows = np.arange(N)[:, None, None] * 8 + np.arange(8)[None, None, :]
    tile_rows = np.broadcast_to(tile_rows, (N, 2, 8)).reshape(-1)
    tile_chan = np.broadcast_to(np.arange(2)[None, :, None], (N, 2, 8)).reshape(-1)
    theta = angles(k_rows[:, :, None], tile_rows[None, None, :])
    same = (chan_of[:, None] == tile_chan[None, :])[None]
    rows = np.concatenate([np.cos(theta) * same, -np.sin(theta) * same], axis=1)
    theta = angles(np.arange(TS)[:, None], np.arange(FRAME)[None, :])
    cos, sin = np.cos(theta), np.sin(theta)
    cols = np.block([[cos, -sin], [sin, cos]])
    theta = angles(np.arange(FRAME)[:, None], PAD + np.arange(FS)[None, :])
    cos, sin = np.cos(theta), np.sin(theta)
    back_cols = np.block([[cos, sin], [-sin, cos]])
    back_rows = np.zeros((FS, N, 2, SLOTS))
    y = PAD + np.arange(FS)
    for m in range(N):
        for slot in range(SLOTS):
            theta = angles(np.int64(ROWS * m + own_row(m, slot)), y)
            back_rows[:, m, 0, slot] = np.cos(theta)
            back_rows[:, m, 1, slot] = -np.sin(theta)
    back_rows[:, N // 2, 0, 0] *= 0.5
    back_rows[:, N // 2, 1, 0] = 0.5
    flip = np.zeros((FRAME, FRAME))
    flip[(FRAME - np.arange(FRAME)) % FRAME, np.arange(FRAME)] = 1.0
    return dict(
        own=half(own),
        mirror=half(mirror),
        rows=half(rows),
        cols=half(cols),
        back_cols=half(back_cols),
        back_rows=half(back_rows.reshape(FS, N * 2 * SLOTS)),
        flip=half(flip),
    )


def channel_at(index):
    return (2 * index - (CHAN - 1)).astype(f32) * (1.0 / CHAN)


def convolve_kernel(
    comps_hbm, weight_hbm, psf_of_hbm, tile_pos_hbm, psf_hbm, mirror_hbm, own_hbm, rows_hbm, cols_hbm, flip_hbm, back_hbm,
    out_ref,
    comps, weight, psf_own, tile_pos, psf, mirror, own, rows, cols, flip, back,
    send_a, recv_a, send_b, model, send_f, psf_of, send_0, far_0, send_m, far,
    psf_sum, turned, row_ph, col_ph, tiles, shifted, prod, send_w,
    local, send_sems, recv_sems, pair_sems,
):
    facet = lax.axis_index("facet")
    freq = lax.axis_index("freq")
    middle = facet == N // 2
    upper = facet >= N // 2
    barrier = pltpu.get_barrier_semaphore()

    def greet(d, _):
        pl.semaphore_signal(barrier, inc=1, device_id={"freq": (freq + d) % N}, device_id_type=MESH)
        pl.semaphore_signal(barrier, inc=1, device_id={"facet": (facet + d) % N}, device_id_type=MESH)
        return 0

    lax.fori_loop(1, N, greet, 0)
    sources = (
        comps_hbm, weight_hbm, psf_of_hbm, psf_hbm, mirror_hbm, tile_pos_hbm,
        own_hbm.at[facet], rows_hbm.at[facet], flip_hbm, cols_hbm, back_hbm,
    )
    targets = (comps, weight, psf_own, psf, mirror, tile_pos, own, rows, flip, cols, back)
    loads = [pltpu.make_async_copy(*pair, local.at[at]) for at, pair in enumerate(zip(sources, targets))]
    for load in loads:
        load.start()

    def copies(at, axis, source, target):
        me = facet if axis == "facet" else freq

        def copy(d, slot):
            return pltpu.make_async_remote_copy(
                src_ref=source, dst_ref=target.at[slot],
                send_sem=send_sems.at[at, d], recv_sem=recv_sems.at[at, slot],
                device_id={axis: (me + d) % N}, device_id_type=MESH,
            )

        def start(d, _):
            copy(d, me).start()
            return 0

        def land(d, _):
            copy(d, (me + N - d) % N).wait_recv()
            return 0

        def leave(d, _):
            copy(d, me).wait_send()
            return 0

        return tuple(functools.partial(lax.fori_loop, 1, N, step, 0) for step in (start, land, leave))

    start_a, land_a, leave_a = copies(0, "freq", send_a, recv_a)
    start_b, land_b, leave_b = copies(1, "facet", send_b, model)
    start_f, land_f, leave_f = copies(2, "facet", send_f, psf_of)

    for load in loads[:3]:
        load.wait()
    send_a[0:64, :] = comps[...]
    row = lax.broadcasted_iota(jnp.int32, (8, 128), 0)
    parts = []
    for c in range(2):
        whole = jnp.full((8, 128), weight[c], f32)
        first = whole.astype(bf16).astype(f32)
        second = (whole - first).astype(bf16).astype(f32)
        third = (whole - first) - second
        parts.append(jnp.where(row == 0, first, jnp.where(row == 1, second, jnp.where(row == 2, third, 0.0))))
    send_a[64:80, :] = jnp.concatenate(parts, axis=0).astype(bf16)
    send_f[...] = jnp.full((16, 128), psf_own[0].astype(f32), f32).astype(bf16)
    recv_a[freq] = send_a[...]
    psf_of[facet] = send_f[...]
    pl.semaphore_wait(barrier, 2 * (N - 1))
    start_a()

    loads[3].wait()
    loads[4].wait()
    for index in range(8):
        both = psf[index // 2, :, index % 2].reshape(2 * ROWS, FRAME)
        send_m[index] = jnp.dot(mirror[...], both, preferred_element_type=f32).astype(bf16)
    copy_m = pltpu.make_async_remote_copy(
        src_ref=send_m, dst_ref=far, send_sem=pair_sems.at[0], recv_sem=pair_sems.at[1],
        device_id={"facet": N - 1 - facet}, device_id_type=MESH,
    )
    copy_m.start()
    send_0[...] = jnp.concatenate(
        [psf[n // 4, n // 2 % 2, n % 2, 0:1].astype(f32) for n in range(16)], axis=0
    ).astype(bf16)
    is_first = 1 - (facet + N - 1) // N
    is_middle = 1 - ((facet + N // 2) % N + N - 1) // N
    copy_0 = pltpu.make_async_remote_copy(
        src_ref=send_0, dst_ref=far_0, send_sem=pair_sems.at[2], recv_sem=pair_sems.at[3],
        device_id={"facet": (N - facet) % N + (N // 2) * (is_first - is_middle)}, device_id_type=MESH,
    )
    copy_0.start()
    start_f()

    for load in loads[5:]:
        load.wait()
    for index in range(8):
        both = psf[index // 2, :, index % 2].reshape(2 * ROWS, FRAME)
        psf_sum[index // 2, index % 2, 0:48] = jnp.dot(own[...], both, preferred_element_type=f32)
    row_ph[...], col_ph[...] = phases(facet, tile_pos)

    land_a()

    def add(q, total):
        total = list(total)
        block = recv_a[q].astype(f32)
        comp = block[0:64].reshape(NTILE, 2, 8, 128)
        for c in range(2):
            x = channel_at(2 * q + c)
            power = jnp.sum(block[64 + 8 * c : 72 + 8 * c], axis=0, keepdims=True)
            for n in range(5):
                if n < 3:
                    total[n] = total[n] + power * comp[:, c]
                total[3 + n] = total[3 + n] + power
                power = power * x
        return tuple(total)

    zeros = tuple(jnp.zeros((NTILE, 8, 128), f32) for _ in range(3)) + tuple(jnp.zeros((1, 128), f32) for _ in range(5))
    m0, m1, m2, g0, g1, g2, g3, g4 = lax.fori_loop(0, N, add, zeros)
    c00 = g2 * g4 - g3 * g3
    c01 = g2 * g3 - g1 * g4
    c02 = g1 * g3 - g2 * g2
    c11 = g0 * g4 - g2 * g2
    c12 = g1 * g2 - g0 * g3
    c22 = g0 * g2 - g1 * g1
    det = g0 * c00 + g1 * c01 + g2 * c02
    a0 = ((c00 * m0 + c01 * m1 + c02 * m2) / det).astype(bf16).astype(f32)
    a1 = ((c01 * m0 + c11 * m1 + c12 * m2) / det).astype(bf16).astype(f32)
    a2 = ((c02 * m0 + c12 * m1 + c22 * m2) / det).astype(bf16).astype(f32)
    both = []
    for c in range(2):
        x = channel_at(2 * freq + c)
        both.append(a0 + a1 * x + a2 * (x * x))
    send_b[...] = jnp.stack(both, axis=1).reshape(64, 128).astype(bf16)
    model[facet] = send_b[...]
    start_b()

    land_f()
    copy_0.wait()
    copy_m.wait()
    row = lax.broadcasted_iota(jnp.int32, (16, FRAME), 0)
    for index in range(8):
        p, ri = index // 2, index % 2
        zero_row = [far_0[4 * p + 2 * c + ri : 4 * p + 2 * c + ri + 1].astype(f32) for c in range(2)]
        zero_rows = jnp.where(row == 0, zero_row[0], jnp.where(row == 8, zero_row[1], 0.0))
        psf_sum[p, ri, 48:64] = zero_rows
        lead = jnp.where(
            (row % 8 == 0) & upper,
            jnp.where(middle, psf_sum[p, ri, 0:16], zero_rows),
            far[index, 0:16].astype(f32),
        )
        turned[index, 0:16] = lead.astype(bf16)
        turned[index, 16:48] = far[index, 16:48]
        turned[index, 48:64] = zero_rows.astype(bf16)

    def turn(index, _):
        p, ri = index // 2, index % 2
        flipped = jnp.dot(turned[index], flip[...], preferred_element_type=f32)
        psf_sum[p, ri] = psf_sum[p, ri] + flipped * (1 - 2 * ri).astype(f32)
        return 0

    lax.fori_loop(0, 8, turn, 0)

    land_b()
    for t in range(NTILE):
        block = model[:, 16 * t : 16 * t + 16, :].reshape(256, 128)
        half_way = jnp.dot(rows[...], block, preferred_element_type=f32).astype(bf16)
        half_way = jnp.concatenate([half_way[0:64], half_way[64:128]], axis=1)
        tiles[t] = jnp.dot(half_way, cols[...], preferred_element_type=f32)

    lane = lax.broadcasted_iota(jnp.int32, (64, 128), 1)
    re, im = slice(0, FRAME), slice(FRAME, 2 * FRAME)

    def copy_w(to, slot):
        return pltpu.make_async_remote_copy(
            src_ref=send_w.at[to], dst_ref=out_ref.at[:, slot], send_sem=send_sems.at[3, to], recv_sem=recv_sems.at[3, slot],
            device_id={"facet": to}, device_id_type=MESH,
        )

    def facet_row(step, _):
        a = (facet // FCOLS + (N - 1 - step)) % FCOLS
        for t in range(NTILE):
            rc = jnp.sum(jnp.where(lane == t * FCOLS + a, row_ph[...], 0.0), axis=1, keepdims=True)
            rs = jnp.sum(jnp.where(lane == t * FCOLS + a + 16, row_ph[...], 0.0), axis=1, keepdims=True)
            tr, ti = tiles[t, :, re], tiles[t, :, im]
            shifted[t, :, re] = rc * tr - rs * ti
            shifted[t, :, im] = rc * ti + rs * tr

        for b in range(FCOLS):
            which = jnp.max(psf_of[a * FCOLS + b].astype(f32))
            pick = [jnp.where(which == p, 1.0, 0.0) for p in range(4)]

            def product(g):
                at = slice(16 * g, 16 * g + 16)
                sr = si = hr = hi = 0.0
                for t in range(NTILE):
                    cc = col_ph[0, t * FCOLS + b : t * FCOLS + b + 1]
                    cs = col_ph[1, t * FCOLS + b : t * FCOLS + b + 1]
                    tr, ti = shifted[t, at, re], shifted[t, at, im]
                    sr = sr + (cc * tr - cs * ti)
                    si = si + (cc * ti + cs * tr)
                for p in range(4):
                    hr = hr + pick[p] * psf_sum[p, 0, at]
                    hi = hi + pick[p] * psf_sum[p, 1, at]
                return sr * hr - si * hi, sr * hi + si * hr

            for g in range(3):
                pr, pi = product(g)
                prod[b, 16 * g : 16 * g + 16, re] = pr.astype(bf16)
                prod[b, 16 * g : 16 * g + 16, im] = pi.astype(bf16)

            @pl.when(middle)
            def _():
                pr, pi = product(0)
                more_r, more_i = product(3)
                prod[b, 0:16, re] = (pr - more_i).astype(bf16)
                prod[b, 0:16, im] = (pi + more_r).astype(bf16)

        w = jnp.dot(prod[...].reshape(FCOLS * 48, 2 * FRAME), back[...], preferred_element_type=f32)
        w = w.reshape(FCOLS, 3, 2, 8, 2 * FS)
        for b in range(FCOLS):
            for c in range(2):
                real = w[b, :, c, :, 0:FS].reshape(SLOTS, FS)
                imag = w[b, :, c, :, FS : 2 * FS].reshape(SLOTS, FS)
                send_w[a * FCOLS + b, c] = jnp.concatenate([real, imag], axis=0).astype(bf16)
        for n in range(FCOLS):
            to = a * FCOLS + (facet + n) % FCOLS

            @pl.when(to != facet)
            def _():
                copy_w(to, facet).start()

        return 0

    lax.fori_loop(0, FCOLS, facet_row, 0)
    for c in range(2):
        out_ref[c, facet] = send_w[facet, c]
    leave_a()
    leave_f()
    leave_b()

    def land_w(d, _):
        copy_w((facet + N - d) % N, (facet + N - d) % N).wait()
        return 0

    lax.fori_loop(1, N, land_w, 0)


def phases(facet, tile_pos):
    def turn(index, offset):
        index = index * offset
        theta = (index - jnp.floor(index * (1.0 / FRAME)) * FRAME) * (2.0 * math.pi / FRAME)
        counted = jnp.where((offset >= 0.0) & (offset <= FRAME - TS), 1.0, 0.0)
        return jnp.cos(theta) * counted, -jnp.sin(theta) * counted

    def offsets(place, dim):
        tile = place // FCOLS % NTILE
        at = jnp.zeros(place.shape, jnp.int32)
        for t in range(NTILE):
            at = jnp.where(tile == t, tile_pos[dim, t], at)
        return (at - place % FCOLS * FS + PAD).astype(f32)

    row = lax.broadcasted_iota(jnp.int32, (64, 128), 0)
    lane = lax.broadcasted_iota(jnp.int32, (64, 128), 1)
    slot = row // 16 * 8 + row % 8
    k = facet * ROWS + jnp.where((slot == 0) & (facet >= N // 2), 0, SLOTS + slot)
    k = jnp.where(row >= 48, 0, k).astype(f32)
    cos, sin = turn(k, offsets(lane, 0))
    rows = jnp.where(lane < 16, cos, sin)
    place = lax.broadcasted_iota(jnp.int32, (16, FRAME), 0)
    l = lax.broadcasted_iota(jnp.int32, (16, FRAME), 1).astype(f32)
    return rows, jnp.stack(turn(l, offsets(place, 1)))


def convolve(*args):
    dma = pltpu.SemaphoreType.DMA
    return pl.pallas_call(
        convolve_kernel,
        out_shape=jax.ShapeDtypeStruct((2, N, 48, FS), bf16),
        in_specs=[HBM] * 11,
        out_specs=VMEM,
        scratch_shapes=[
            pltpu.VMEM((64, 128), bf16),
            pltpu.SMEM((2,), f32),
            pltpu.SMEM((1,), jnp.int32),
            pltpu.SMEM((2, NTILE), jnp.int32),
            pltpu.VMEM((4, 2, 2, ROWS, FRAME), bf16),
            pltpu.VMEM((48, 96), bf16),
            pltpu.VMEM((48, 96), bf16),
            pltpu.VMEM((128, 256), bf16),
            pltpu.VMEM((256, 2 * FRAME), bf16),
            pltpu.VMEM((FRAME, FRAME), bf16),
            pltpu.VMEM((2 * FRAME, 2 * FS), bf16),
            pltpu.VMEM((80, 128), bf16),
            pltpu.VMEM((N, 80, 128), bf16),
            pltpu.VMEM((64, 128), bf16),
            pltpu.VMEM((N, 64, 128), bf16),
            pltpu.VMEM((16, 128), bf16),
            pltpu.VMEM((N, 16, 128), bf16),
            pltpu.VMEM((16, FRAME), bf16),
            pltpu.VMEM((16, FRAME), bf16),
            pltpu.VMEM((8, 48, FRAME), bf16),
            pltpu.VMEM((8, 48, FRAME), bf16),
            pltpu.VMEM((4, 2, 64, FRAME), f32),
            pltpu.VMEM((8, 64, FRAME), bf16),
            pltpu.VMEM((64, 128), f32),
            pltpu.VMEM((2, 16, FRAME), f32),
            pltpu.VMEM((NTILE, 64, 2 * FRAME), f32),
            pltpu.VMEM((NTILE, 64, 2 * FRAME), f32),
            pltpu.VMEM((FCOLS, 48, 2 * FRAME), bf16),
            pltpu.VMEM((N, 2, 48, FS), bf16),
            dma((11,)), dma((4, N)), dma((4, N)), dma((4,)),
        ],
        compiler_params=pltpu.CompilerParams(collective_id=0, has_side_effects=True, vmem_limit_bytes=56 * MIB),
        name="convolve",
    )(*args)


def rows_kernel(residual_ref, w_ref, back_ref, out_ref):
    convolved = jnp.dot(back_ref[...], w_ref[0], preferred_element_type=f32)
    out_ref[0, 0] = residual_ref[0, 0] - convolved * (1.0 / (FRAME * FRAME))


def subtract(residual, w, back):
    return pl.pallas_call(
        rows_kernel,
        grid=(2,),
        out_shape=jax.ShapeDtypeStruct(residual.shape, f32),
        in_specs=[
            pl.BlockSpec((1, 1, FS, FS), lambda c: (c, 0, 0, 0)),
            pl.BlockSpec((1, FRAME, FS), lambda c: (c, 0, 0)),
            pl.BlockSpec((FS, FRAME), lambda c: (0, 0)),
        ],
        out_specs=pl.BlockSpec((1, 1, FS, FS), lambda c: (c, 0, 0, 0)),
        compiler_params=pltpu.CompilerParams(vmem_limit_bytes=24 * MIB),
        name="subtract",
    )(residual, w, back)


def shards(residual, components, chan_weight, tile_pos, facet_psf, psf_spectra):
    table = {name: jnp.asarray(value) for name, value in tables().items()}
    w = convolve(
        components.reshape(64, 128), chan_weight, facet_psf, tile_pos.T, psf_spectra,
        *(table[name] for name in ("mirror", "own", "rows", "cols", "flip", "back_cols")),
    )
    return subtract(residual, w.reshape(2, FRAME, FS), table["back_rows"])


def solution(mesh):
    placed = (
        P("freq", "facet", None, None),
        P(None, "freq", "facet", None),
        P("freq"),
        P(),
        P("facet"),
        P(None, "freq", None, "facet", None),
    )
    return jax.shard_map(
        shards,
        mesh=mesh,
        in_specs=placed,
        out_specs=P("freq", "facet", None, None),
        check_vma=False,
    )
```

```python
import functools
import math

import jax
import jax.numpy as jnp
import ml_dtypes
import numpy as np
from jax import lax
from jax.experimental import pallas as pl
from jax.experimental.pallas import tpu as pltpu
from jax.sharding import PartitionSpec as P

CHAN = 32
FS = 512
PAD = 128
TS = 128
NTILE = 4
FCOLS = 4
FRAME = 768
N = 16
ROWS = 48
SLOTS = 24
MIB = 1 << 20
MESH = pl.DeviceIdType.MESH
VMEM = pl.BlockSpec(memory_space=pltpu.VMEM)
HBM = pl.BlockSpec(memory_space=pltpu.HBM)
f32 = jnp.float32
bf16 = jnp.bfloat16


def own_row(m, slot):
    return 0 if slot == 0 and m >= N // 2 else SLOTS + slot


def angles(left, right):
    return (left * right % FRAME).astype(np.float64) * (2.0 * math.pi / FRAME)


def half(table):
    return table.astype(ml_dtypes.bfloat16)


@functools.cache
def tables():
    chan_of = np.arange(64) // 32
    k_rows = np.zeros((N, 64), np.int64)
    own = np.zeros((N, 48, 96))
    mirror = np.zeros((48, 96))
    for m in range(N):
        for c in range(2):
            for slot in range(SLOTS):
                k_rows[m, 32 * c + slot] = ROWS * m + own_row(m, slot)
                own[m, SLOTS * c + slot, ROWS * c + own_row(m, slot)] = 1.0
    for c in range(2):
        for slot in range(SLOTS):
            mirror[SLOTS * c + slot, ROWS * c + SLOTS - slot] = 1.0
    tile_rows = np.arange(N)[:, None, None] * 8 + np.arange(8)[None, None, :]
    tile_rows = np.broadcast_to(tile_rows, (N, 2, 8)).reshape(-1)
    tile_chan = np.broadcast_to(np.arange(2)[None, :, None], (N, 2, 8)).reshape(-1)
    theta = angles(k_rows[:, :, None], tile_rows[None, None, :])
    same = (chan_of[:, None] == tile_chan[None, :])[None]
    rows = np.concatenate([np.cos(theta) * same, -np.sin(theta) * same], axis=1)
    theta = angles(np.arange(TS)[:, None], np.arange(FRAME)[None, :])
    cos, sin = np.cos(theta), np.sin(theta)
    cols = np.block([[cos, -sin], [sin, cos]])
    theta = angles(np.arange(FRAME)[:, None], PAD + np.arange(FS)[None, :])
    cos, sin = np.cos(theta), np.sin(theta)
    back_cols = np.block([[cos, sin], [-sin, cos]])
    back_rows = np.zeros((FS, N, 2, SLOTS))
    y = PAD + np.arange(FS)
    for m in range(N):
        for slot in range(SLOTS):
            theta = angles(np.int64(ROWS * m + own_row(m, slot)), y)
            back_rows[:, m, 0, slot] = np.cos(theta)
            back_rows[:, m, 1, slot] = -np.sin(theta)
    back_rows[:, N // 2, 0, 0] *= 0.5
    back_rows[:, N // 2, 1, 0] = 0.5
    flip = np.zeros((FRAME, FRAME))
    flip[(FRAME - np.arange(FRAME)) % FRAME, np.arange(FRAME)] = 1.0
    return dict(
        own=half(own),
        mirror=half(mirror),
        rows=half(rows),
        cols=half(cols),
        back_cols=half(back_cols),
        back_rows=half(back_rows.reshape(FS, N * 2 * SLOTS)),
        flip=half(flip),
    )


def channel_at(index):
    return (2 * index - (CHAN - 1)).astype(f32) * (1.0 / CHAN)


def convolve_kernel(
    comps_hbm, weight_hbm, psf_of_hbm, tile_pos_hbm, psf_hbm, mirror_hbm, own_hbm, rows_hbm, cols_hbm, flip_hbm, back_hbm,
    out_ref,
    comps, weight, psf_own, tile_pos, psf, mirror, own, rows, cols, flip, back,
    send_a, recv_a, send_b, model, send_f, psf_of, send_0, far_0, send_m, far,
    psf_sum, turned, row_ph, col_ph, tiles, shifted, prod, send_w,
    local, send_sems, recv_sems, pair_sems,
):
    facet = lax.axis_index("facet")
    freq = lax.axis_index("freq")
    middle = facet == N // 2
    upper = facet >= N // 2
    barrier = pltpu.get_barrier_semaphore()

    def greet(d, _):
        pl.semaphore_signal(barrier, inc=1, device_id={"freq": (freq + d) % N}, device_id_type=MESH)
        pl.semaphore_signal(barrier, inc=1, device_id={"facet": (facet + d) % N}, device_id_type=MESH)
        return 0

    lax.fori_loop(1, N, greet, 0)
    sources = (
        comps_hbm, weight_hbm, psf_of_hbm, psf_hbm, mirror_hbm, flip_hbm,
        own_hbm.at[facet], rows_hbm.at[facet], tile_pos_hbm, cols_hbm, back_hbm,
    )
    targets = (comps, weight, psf_own, psf, mirror, flip, own, rows, tile_pos, cols, back)
    loads = [pltpu.make_async_copy(*pair, local.at[at]) for at, pair in enumerate(zip(sources, targets))]
    for load in loads:
        load.start()

    def copies(at, axis, source, target):
        me = facet if axis == "facet" else freq

        def copy(d, slot):
            return pltpu.make_async_remote_copy(
                src_ref=source, dst_ref=target.at[slot],
                send_sem=send_sems.at[at, d], recv_sem=recv_sems.at[at, slot],
                device_id={axis: (me + d) % N}, device_id_type=MESH,
            )

        def start(d, _):
            copy(d, me).start()
            return 0

        def land(d, _):
            copy(d, (me + N - d) % N).wait_recv()
            return 0

        def leave(d, _):
            copy(d, me).wait_send()
            return 0

        return tuple(functools.partial(lax.fori_loop, 1, N, step, 0) for step in (start, land, leave))

    start_a, land_a, leave_a = copies(0, "freq", send_a, recv_a)
    start_b, land_b, leave_b = copies(1, "facet", send_b, model)
    start_f, land_f, leave_f = copies(2, "facet", send_f, psf_of)

    for load in loads[:3]:
        load.wait()
    send_a[0:64, :] = comps[...]
    row = lax.broadcasted_iota(jnp.int32, (8, 128), 0)
    parts = []
    for c in range(2):
        whole = jnp.full((8, 128), weight[c], f32)
        first = whole.astype(bf16).astype(f32)
        second = (whole - first).astype(bf16).astype(f32)
        third = (whole - first) - second
        parts.append(jnp.where(row == 0, first, jnp.where(row == 1, second, jnp.where(row == 2, third, 0.0))))
    send_a[64:80, :] = jnp.concatenate(parts, axis=0).astype(bf16)
    send_f[...] = jnp.full((16, 128), psf_own[0].astype(f32), f32).astype(bf16)
    recv_a[freq] = send_a[...]
    psf_of[facet] = send_f[...]

    loads[3].wait()
    loads[4].wait()
    loads[5].wait()
    for p in range(4):
        parts = [
            jnp.dot(mirror[...], psf[p, :, ri].reshape(2 * ROWS, FRAME), preferred_element_type=f32) for ri in range(2)
        ]
        for c in range(2):
            part = jnp.concatenate([part[SLOTS * c : SLOTS * (c + 1)] for part in parts], axis=0)
            turned[c, 48 * p : 48 * (p + 1)] = part.astype(bf16)
    send_m[...] = (
        jnp.dot(turned[...].reshape(8 * 48, FRAME), flip[...], preferred_element_type=f32)
        .astype(bf16)
        .reshape(2, 4 * 48, FRAME)
    )
    send_0[...] = jnp.concatenate(
        [psf[n // 4, n // 2 % 2, n % 2, 0:1].astype(f32) for n in range(16)], axis=0
    ).astype(bf16)
    copies_m = [
        pltpu.make_async_remote_copy(
            src_ref=send_m.at[c], dst_ref=far.at[c], send_sem=pair_sems.at[2 + c], recv_sem=pair_sems.at[4 + c],
            device_id={"facet": N - 1 - facet}, device_id_type=MESH,
        )
        for c in range(2)
    ]
    is_first = 1 - (facet + N - 1) // N
    is_middle = 1 - ((facet + N // 2) % N + N - 1) // N
    copy_0 = pltpu.make_async_remote_copy(
        src_ref=send_0, dst_ref=far_0, send_sem=pair_sems.at[0], recv_sem=pair_sems.at[1],
        device_id={"facet": (N - facet) % N + (N // 2) * (is_first - is_middle)}, device_id_type=MESH,
    )
    pl.semaphore_wait(barrier, 2 * (N - 1))
    copies_m[0].start()
    start_a()
    copy_0.start()
    start_f()

    for load in loads[6:]:
        load.wait()
    for index in range(8):
        both = psf[index // 2, :, index % 2].reshape(2 * ROWS, FRAME)
        chosen = jnp.dot(own[...], both, preferred_element_type=f32)
        for c in range(2):
            psf_sum[c, index // 2, index % 2, 0:SLOTS] = chosen[SLOTS * c : SLOTS * (c + 1)]
    row_ph[...], col_ph[...] = phases(facet, tile_pos)

    copy_0.wait()
    lead_row = lax.broadcasted_iota(jnp.int32, (8, FRAME), 0) == 0
    zeros_there = far_0[...].astype(f32)
    ends = jnp.dot(jnp.concatenate([far_0[...], send_0[...]], axis=0), flip[...], preferred_element_type=f32)
    for n in range(16):
        p, c, ri = n // 4, n // 2 % 2, n % 2
        sign = 1.0 - 2.0 * ri
        there, here = ends[n : n + 1], ends[16 + n : 17 + n]
        psf_sum[c, p, ri, 24:32] = jnp.where(lead_row, zeros_there[n : n + 1] + sign * there, 0.0)
        lead = jnp.where(lead_row & upper, jnp.where(middle, here, there), 0.0)
        psf_sum[c, p, ri, 0:8] = psf_sum[c, p, ri, 0:8] + sign * lead

    land_a()

    def add(q, total):
        total = list(total)
        block = recv_a[q].astype(f32)
        comp = block[0:64].reshape(NTILE, 2, 8, 128)
        for c in range(2):
            x = channel_at(2 * q + c)
            power = jnp.sum(block[64 + 8 * c : 72 + 8 * c], axis=0, keepdims=True)
            for n in range(5):
                if n < 3:
                    total[n] = total[n] + power * comp[:, c]
                total[3 + n] = total[3 + n] + power
                power = power * x
        return tuple(total)

    zeros = tuple(jnp.zeros((NTILE, 8, 128), f32) for _ in range(3)) + tuple(jnp.zeros((1, 128), f32) for _ in range(5))
    m0, m1, m2, g0, g1, g2, g3, g4 = lax.fori_loop(0, N, add, zeros)
    c00 = g2 * g4 - g3 * g3
    c01 = g2 * g3 - g1 * g4
    c02 = g1 * g3 - g2 * g2
    c11 = g0 * g4 - g2 * g2
    c12 = g1 * g2 - g0 * g3
    c22 = g0 * g2 - g1 * g1
    det = g0 * c00 + g1 * c01 + g2 * c02
    a0 = ((c00 * m0 + c01 * m1 + c02 * m2) / det).astype(bf16).astype(f32)
    a1 = ((c01 * m0 + c11 * m1 + c12 * m2) / det).astype(bf16).astype(f32)
    a2 = ((c02 * m0 + c12 * m1 + c22 * m2) / det).astype(bf16).astype(f32)
    both = []
    for c in range(2):
        x = channel_at(2 * freq + c)
        both.append(a0 + a1 * x + a2 * (x * x))
    send_b[...] = jnp.stack(both, axis=1).reshape(64, 128).astype(bf16)
    model[facet] = send_b[...]
    start_b()

    land_b()
    copies_m[1].start()
    for t in range(NTILE):
        block = model[:, 16 * t : 16 * t + 16, :].reshape(256, 128)
        half_way = jnp.dot(rows[...], block, preferred_element_type=f32).astype(bf16)
        half_way = jnp.concatenate([half_way[0:64], half_way[64:128]], axis=1)
        tiles[t] = jnp.dot(half_way, cols[...], preferred_element_type=f32)

    lane = lax.broadcasted_iota(jnp.int32, (32, 128), 1)
    re, im = slice(0, FRAME), slice(FRAME, 2 * FRAME)

    def copy_w(c, to, slot):
        return pltpu.make_async_remote_copy(
            src_ref=send_w.at[c, to], dst_ref=out_ref.at[c, slot],
            send_sem=send_sems.at[3 + c, to], recv_sem=recv_sems.at[3 + c, slot],
            device_id={"facet": to}, device_id_type=MESH,
        )

    def facet_row(c, step):
        a = (facet // FCOLS + (N - 1 - step)) % FCOLS
        base = 32 * c
        for t in range(NTILE):
            phase = row_ph[base : base + 32]
            rc = jnp.sum(jnp.where(lane == t * FCOLS + a, phase, 0.0), axis=1, keepdims=True)
            rs = jnp.sum(jnp.where(lane == t * FCOLS + a + 16, phase, 0.0), axis=1, keepdims=True)
            tr, ti = tiles[t, base : base + 32, re], tiles[t, base : base + 32, im]
            shifted[t, :, re] = rc * tr - rs * ti
            shifted[t, :, im] = rc * ti + rs * tr

        for pair in range(2):
            picks = []
            for b in (2 * pair, 2 * pair + 1):
                which = jnp.max(psf_of[a * FCOLS + b].astype(f32))
                picks.append([jnp.where(which == p, 1.0, 0.0) for p in range(4)])

            def product(half, g):
                b = 2 * pair + half
                at = slice(8 * g, 8 * g + 8)
                sr = si = hr = hi = 0.0
                for t in range(NTILE):
                    cc = col_ph[0, t * FCOLS + b : t * FCOLS + b + 1]
                    cs = col_ph[1, t * FCOLS + b : t * FCOLS + b + 1]
                    tr, ti = shifted[t, at, re], shifted[t, at, im]
                    sr = sr + (cc * tr - cs * ti)
                    si = si + (cc * ti + cs * tr)
                for p in range(4):
                    hr = hr + picks[half][p] * psf_sum[c, p, 0, at]
                    hi = hi + picks[half][p] * psf_sum[c, p, 1, at]
                return sr * hr - si * hi, sr * hi + si * hr

            for n in range(3):
                low, high = (product((2 * n + m) // 3, (2 * n + m) % 3) for m in range(2))
                at = slice(48 * pair + 16 * n, 48 * pair + 16 * n + 16)
                prod[at, re] = jnp.concatenate([low[0], high[0]], axis=0).astype(bf16)
                prod[at, im] = jnp.concatenate([low[1], high[1]], axis=0).astype(bf16)

            @pl.when(middle)
            def _():
                for half in range(2):
                    at = slice(48 * pair + 16 * half, 48 * pair + 16 * half + 16)
                    pr, pi = product(half, 0)
                    more_r, more_i = product(half, 3)
                    lead, near = (pr - more_i, pi + more_r), product(0, 1 + half)
                    low, high = (lead, near) if half == 0 else (near, lead)
                    prod[at, re] = jnp.concatenate([low[0], high[0]], axis=0).astype(bf16)
                    prod[at, im] = jnp.concatenate([low[1], high[1]], axis=0).astype(bf16)

        w = jnp.dot(prod[...], back[...], preferred_element_type=f32)
        for b in range(FCOLS):
            part = w[SLOTS * b : SLOTS * (b + 1)]
            both = jnp.concatenate([part[:, 0:FS], part[:, FS : 2 * FS]], axis=0)
            send_w[c, a * FCOLS + b] = both.astype(bf16)
        for n in range(FCOLS):
            to = a * FCOLS + (facet + n) % FCOLS

            @pl.when(to != facet)
            def _():
                copy_w(c, to, facet).start()

    land_f()
    for c in range(2):
        copies_m[c].wait()
        for index in range(8):
            if index % 2 == 0:
                values = far[c, 24 * index : 24 * index + 48].astype(f32)
            value = values[24 * (index % 2) : 24 * (index % 2) + 24]
            p, ri = index // 2, index % 2
            sign = 1.0 - 2.0 * ri
            lead = jnp.where(lead_row & upper, 0.0, value[0:8])
            psf_sum[c, p, ri, 0:8] = psf_sum[c, p, ri, 0:8] + sign * lead
            psf_sum[c, p, ri, 8:24] = psf_sum[c, p, ri, 8:24] + sign * value[8:24]

        def row_step(step, _):
            facet_row(c, step)
            return 0

        lax.fori_loop(0, FCOLS, row_step, 0)
        out_ref[c, facet] = send_w[c, facet]
    leave_a()
    leave_f()
    leave_b()

    def land_w(d, _):
        for c in range(2):
            copy_w(c, (facet + N - d) % N, (facet + N - d) % N).wait()
        return 0

    lax.fori_loop(1, N, land_w, 0)


def phases(facet, tile_pos):
    def turn(index, offset):
        index = index * offset
        theta = (index - jnp.floor(index * (1.0 / FRAME)) * FRAME) * (2.0 * math.pi / FRAME)
        counted = jnp.where((offset >= 0.0) & (offset <= FRAME - TS), 1.0, 0.0)
        return jnp.cos(theta) * counted, -jnp.sin(theta) * counted

    def offsets(place, dim):
        tile = place // FCOLS % NTILE
        at = jnp.zeros(place.shape, jnp.int32)
        for t in range(NTILE):
            at = jnp.where(tile == t, tile_pos[dim, t], at)
        return (at - place % FCOLS * FS + PAD).astype(f32)

    row = lax.broadcasted_iota(jnp.int32, (64, 128), 0)
    lane = lax.broadcasted_iota(jnp.int32, (64, 128), 1)
    slot = row % 32
    k = facet * ROWS + jnp.where((slot == 0) & (facet >= N // 2), 0, SLOTS + slot)
    k = jnp.where(slot >= SLOTS, 0, k).astype(f32)
    cos, sin = turn(k, offsets(lane, 0))
    rows = jnp.where(lane < 16, cos, sin)
    place = lax.broadcasted_iota(jnp.int32, (16, FRAME), 0)
    l = lax.broadcasted_iota(jnp.int32, (16, FRAME), 1).astype(f32)
    return rows, jnp.stack(turn(l, offsets(place, 1)))


def convolve(*args):
    dma = pltpu.SemaphoreType.DMA
    return pl.pallas_call(
        convolve_kernel,
        out_shape=jax.ShapeDtypeStruct((2, N, 48, FS), bf16),
        in_specs=[HBM] * 11,
        out_specs=VMEM,
        scratch_shapes=[
            pltpu.VMEM((64, 128), bf16),
            pltpu.SMEM((2,), f32),
            pltpu.SMEM((1,), jnp.int32),
            pltpu.SMEM((2, NTILE), jnp.int32),
            pltpu.VMEM((4, 2, 2, ROWS, FRAME), bf16),
            pltpu.VMEM((48, 96), bf16),
            pltpu.VMEM((48, 96), bf16),
            pltpu.VMEM((128, 256), bf16),
            pltpu.VMEM((256, 2 * FRAME), bf16),
            pltpu.VMEM((FRAME, FRAME), bf16),
            pltpu.VMEM((2 * FRAME, 2 * FS), bf16),
            pltpu.VMEM((80, 128), bf16),
            pltpu.VMEM((N, 80, 128), bf16),
            pltpu.VMEM((64, 128), bf16),
            pltpu.VMEM((N, 64, 128), bf16),
            pltpu.VMEM((16, 128), bf16),
            pltpu.VMEM((N, 16, 128), bf16),
            pltpu.VMEM((16, FRAME), bf16),
            pltpu.VMEM((16, FRAME), bf16),
            pltpu.VMEM((2, 4 * 48, FRAME), bf16),
            pltpu.VMEM((2, 4 * 48, FRAME), bf16),
            pltpu.VMEM((2, 4, 2, 32, FRAME), f32),
            pltpu.VMEM((2, 4 * 48, FRAME), bf16),
            pltpu.VMEM((64, 128), f32),
            pltpu.VMEM((2, 16, FRAME), f32),
            pltpu.VMEM((NTILE, 64, 2 * FRAME), f32),
            pltpu.VMEM((NTILE, 32, 2 * FRAME), f32),
            pltpu.VMEM((FCOLS * SLOTS, 2 * FRAME), bf16),
            pltpu.VMEM((2, N, 48, FS), bf16),
            dma((11,)), dma((5, N)), dma((5, N)), dma((6,)),
        ],
        compiler_params=pltpu.CompilerParams(collective_id=0, has_side_effects=True, vmem_limit_bytes=56 * MIB),
        name="convolve",
    )(*args)


def rows_kernel(residual_ref, w_ref, back_ref, out_ref):
    convolved = jnp.dot(back_ref[...], w_ref[0], preferred_element_type=f32)
    out_ref[0, 0] = residual_ref[0, 0] - convolved * (1.0 / (FRAME * FRAME))


def subtract(residual, w, back):
    return pl.pallas_call(
        rows_kernel,
        grid=(2,),
        out_shape=jax.ShapeDtypeStruct(residual.shape, f32),
        in_specs=[
            pl.BlockSpec((1, 1, FS, FS), lambda c: (c, 0, 0, 0)),
            pl.BlockSpec((1, FRAME, FS), lambda c: (c, 0, 0)),
            pl.BlockSpec((FS, FRAME), lambda c: (0, 0)),
        ],
        out_specs=pl.BlockSpec((1, 1, FS, FS), lambda c: (c, 0, 0, 0)),
        compiler_params=pltpu.CompilerParams(vmem_limit_bytes=24 * MIB),
        name="subtract",
    )(residual, w, back)


def shards(residual, components, chan_weight, tile_pos, facet_psf, psf_spectra):
    table = {name: jnp.asarray(value) for name, value in tables().items()}
    w = convolve(
        components.reshape(64, 128), chan_weight, facet_psf, tile_pos.T, psf_spectra,
        *(table[name] for name in ("mirror", "own", "rows", "cols", "flip", "back_cols")),
    )
    return subtract(residual, w.reshape(2, FRAME, FS), table["back_rows"])


def solution(mesh):
    placed = (
        P("freq", "facet", None, None),
        P(None, "freq", "facet", None),
        P("freq"),
        P(),
        P("facet"),
        P(None, "freq", None, "facet", None),
    )
    return jax.shard_map(
        shards,
        mesh=mesh,
        in_specs=placed,
        out_specs=P("freq", "facet", None, None),
        check_vma=False,
    )
```

```python
import functools
import math

import jax
import jax.numpy as jnp
import ml_dtypes
import numpy as np
from jax import lax
from jax.experimental import pallas as pl
from jax.experimental.pallas import tpu as pltpu
from jax.sharding import PartitionSpec as P

CHAN = 32
FS = 512
PAD = 128
TS = 128
NTILE = 4
FCOLS = 4
FRAME = 768
N = 16
ROWS = 48
AHEAD = 48
SLOTS = 24
MIB = 1 << 20
MESH = pl.DeviceIdType.MESH
VMEM = pl.BlockSpec(memory_space=pltpu.VMEM)
HBM = pl.BlockSpec(memory_space=pltpu.HBM)
f32 = jnp.float32
bf16 = jnp.bfloat16


def own_row(m, slot):
    return 0 if slot == 0 and m >= N // 2 else SLOTS + slot


def angles(left, right):
    return (left * right % FRAME).astype(np.float64) * (2.0 * math.pi / FRAME)


def half(table):
    return table.astype(ml_dtypes.bfloat16)


@functools.cache
def tables():
    chan_of = np.arange(64) // 32
    k_rows = np.zeros((N, 64), np.int64)
    own = np.zeros((N, 48, 96))
    mirror = np.zeros((48, 96))
    for m in range(N):
        for c in range(2):
            for slot in range(SLOTS):
                k_rows[m, 32 * c + slot] = ROWS * m + own_row(m, slot)
                own[m, SLOTS * c + slot, ROWS * c + own_row(m, slot)] = 1.0
    for c in range(2):
        for slot in range(SLOTS):
            mirror[SLOTS * c + slot, ROWS * c + SLOTS - slot] = 1.0
    tile_rows = np.arange(N)[:, None, None] * 8 + np.arange(8)[None, None, :]
    tile_rows = np.broadcast_to(tile_rows, (N, 2, 8)).reshape(-1)
    tile_chan = np.broadcast_to(np.arange(2)[None, :, None], (N, 2, 8)).reshape(-1)
    theta = angles(k_rows[:, :, None], tile_rows[None, None, :])
    same = (chan_of[:, None] == tile_chan[None, :])[None]
    rows = np.concatenate([np.cos(theta) * same, -np.sin(theta) * same], axis=1)
    theta = angles(np.arange(TS)[:, None], np.arange(FRAME)[None, :])
    cos, sin = np.cos(theta), np.sin(theta)
    cols = np.block([[cos, -sin], [sin, cos]])
    theta = angles(np.arange(FRAME)[:, None], PAD + np.arange(FS)[None, :])
    cos, sin = np.cos(theta), np.sin(theta)
    back_cols = np.block([[cos, sin], [-sin, cos]])
    back_rows = np.zeros((FS, N, 2, SLOTS))
    y = PAD + np.arange(FS)
    for m in range(N):
        for slot in range(SLOTS):
            theta = angles(np.int64(ROWS * m + own_row(m, slot)), y)
            back_rows[:, m, 0, slot] = np.cos(theta)
            back_rows[:, m, 1, slot] = -np.sin(theta)
    back_rows[:, N // 2, 0, 0] *= 0.5
    back_rows[:, N // 2, 1, 0] = 0.5
    flip = np.zeros((FRAME, FRAME))
    flip[(FRAME - np.arange(FRAME)) % FRAME, np.arange(FRAME)] = 1.0
    return dict(
        own=half(own),
        mirror=half(mirror),
        rows=half(rows),
        cols=half(cols),
        back_cols=half(back_cols),
        back_rows=half(back_rows.reshape(FS, N * 2 * SLOTS)),
        flip=half(flip),
    )


def channel_at(index):
    return (2 * index - (CHAN - 1)).astype(f32) * (1.0 / CHAN)


def convolve_kernel(
    comps_hbm, weight_hbm, psf_of_hbm, tile_pos_hbm, psf_hbm, mirror_hbm, own_hbm, rows_hbm, cols_hbm, flip_hbm, back_hbm,
    out_ref,
    comps, weight, psf_own, tile_pos, psf, mirror, own, rows, cols, flip, back,
    send_a, recv_a, send_b, model, send_f, psf_of, send_0, far_0, send_m, far,
    psf_sum, turned, row_ph, col_ph, tiles, shifted, prod, send_w,
    local, send_sems, recv_sems, pair_sems,
):
    facet = lax.axis_index("facet")
    freq = lax.axis_index("freq")
    middle = facet == N // 2
    upper = facet >= N // 2
    barrier = pltpu.get_barrier_semaphore()

    def greet(d, _):
        pl.semaphore_signal(barrier, inc=1, device_id={"freq": (freq + d) % N}, device_id_type=MESH)
        pl.semaphore_signal(barrier, inc=1, device_id={"facet": (facet + d) % N}, device_id_type=MESH)
        return 0

    lax.fori_loop(1, N, greet, 0)
    sources = (
        comps_hbm, weight_hbm, psf_of_hbm, psf_hbm, mirror_hbm, flip_hbm,
        own_hbm.at[facet], rows_hbm.at[facet], tile_pos_hbm, cols_hbm, back_hbm,
    )
    targets = (comps, weight, psf_own, psf, mirror, flip, own, rows, tile_pos, cols, back)
    loads = [pltpu.make_async_copy(*pair, local.at[at]) for at, pair in enumerate(zip(sources, targets))]
    for load in loads:
        load.start()

    def copies(at, axis, source, target):
        me = facet if axis == "facet" else freq

        def copy(d, slot):
            return pltpu.make_async_remote_copy(
                src_ref=source, dst_ref=target.at[slot],
                send_sem=send_sems.at[at, d], recv_sem=recv_sems.at[at, slot],
                device_id={axis: (me + d) % N}, device_id_type=MESH,
            )

        def start(d, _):
            copy(d, me).start()
            return 0

        def land(d, _):
            copy(d, (me + N - d) % N).wait_recv()
            return 0

        def leave(d, _):
            copy(d, me).wait_send()
            return 0

        return tuple(functools.partial(lax.fori_loop, 1, N, step, 0) for step in (start, land, leave))

    start_a, land_a, leave_a = copies(0, "freq", send_a, recv_a)
    start_b, land_b, leave_b = copies(1, "facet", send_b, model)
    start_f, land_f, leave_f = copies(2, "facet", send_f, psf_of)

    for load in loads[:3]:
        load.wait()
    send_a[0:64, :] = comps[...]
    row = lax.broadcasted_iota(jnp.int32, (8, 128), 0)
    parts = []
    for c in range(2):
        whole = jnp.full((8, 128), weight[c], f32)
        first = whole.astype(bf16).astype(f32)
        second = (whole - first).astype(bf16).astype(f32)
        third = (whole - first) - second
        parts.append(jnp.where(row == 0, first, jnp.where(row == 1, second, jnp.where(row == 2, third, 0.0))))
    send_a[64:80, :] = jnp.concatenate(parts, axis=0).astype(bf16)
    send_f[...] = jnp.full((16, 128), psf_own[0].astype(f32), f32).astype(bf16)
    recv_a[freq] = send_a[...]
    psf_of[facet] = send_f[...]

    loads[3].wait()
    loads[4].wait()
    loads[5].wait()
    for p in range(4):
        parts = [
            jnp.dot(mirror[...], psf[p, :, ri].reshape(2 * ROWS, FRAME), preferred_element_type=f32) for ri in range(2)
        ]
        for c in range(2):
            part = jnp.concatenate([part[SLOTS * c : SLOTS * (c + 1)] for part in parts], axis=0)
            turned[c, 48 * p : 48 * (p + 1)] = part.astype(bf16)
    send_m[...] = (
        jnp.dot(turned[...].reshape(8 * 48, FRAME), flip[...], preferred_element_type=f32)
        .astype(bf16)
        .reshape(2, 4 * 48, FRAME)
    )
    send_0[...] = jnp.concatenate(
        [psf[n // 4, n // 2 % 2, n % 2, 0:1].astype(f32) for n in range(16)], axis=0
    ).astype(bf16)
    copies_m = [
        pltpu.make_async_remote_copy(
            src_ref=send_m.at[c, part], dst_ref=far.at[c, part],
            send_sem=pair_sems.at[2 + at], recv_sem=pair_sems.at[5 + at],
            device_id={"facet": N - 1 - facet}, device_id_type=MESH,
        )
        for at, (c, part) in enumerate(
            ((0, pl.ds(0, 192)), (1, pl.ds(0, AHEAD)), (1, pl.ds(AHEAD, 192 - AHEAD)))
        )
    ]
    is_first = 1 - (facet + N - 1) // N
    is_middle = 1 - ((facet + N // 2) % N + N - 1) // N
    copy_0 = pltpu.make_async_remote_copy(
        src_ref=send_0, dst_ref=far_0, send_sem=pair_sems.at[0], recv_sem=pair_sems.at[1],
        device_id={"facet": (N - facet) % N + (N // 2) * (is_first - is_middle)}, device_id_type=MESH,
    )
    pl.semaphore_wait(barrier, 2 * (N - 1))
    copies_m[0].start()
    start_a()
    copy_0.start()
    copies_m[1].start()
    start_f()

    for load in loads[6:]:
        load.wait()
    for index in range(8):
        both = psf[index // 2, :, index % 2].reshape(2 * ROWS, FRAME)
        chosen = jnp.dot(own[...], both, preferred_element_type=f32)
        for c in range(2):
            psf_sum[c, index // 2, index % 2, 0:SLOTS] = chosen[SLOTS * c : SLOTS * (c + 1)]
    row_ph[...], col_ph[...] = phases(facet, tile_pos)

    copy_0.wait()
    lead_row = lax.broadcasted_iota(jnp.int32, (8, FRAME), 0) == 0
    zeros_there = far_0[...].astype(f32)
    ends = jnp.dot(jnp.concatenate([far_0[...], send_0[...]], axis=0), flip[...], preferred_element_type=f32)
    for n in range(16):
        p, c, ri = n // 4, n // 2 % 2, n % 2
        sign = 1.0 - 2.0 * ri
        there, here = ends[n : n + 1], ends[16 + n : 17 + n]
        psf_sum[c, p, ri, 24:32] = jnp.where(lead_row, zeros_there[n : n + 1] + sign * there, 0.0)
        lead = jnp.where(lead_row & upper, jnp.where(middle, here, there), 0.0)
        psf_sum[c, p, ri, 0:8] = psf_sum[c, p, ri, 0:8] + sign * lead

    land_a()

    def add(q, total):
        total = list(total)
        block = recv_a[q].astype(f32)
        comp = block[0:64].reshape(NTILE, 2, 8, 128)
        for c in range(2):
            x = channel_at(2 * q + c)
            power = jnp.sum(block[64 + 8 * c : 72 + 8 * c], axis=0, keepdims=True)
            for n in range(5):
                if n < 3:
                    total[n] = total[n] + power * comp[:, c]
                total[3 + n] = total[3 + n] + power
                power = power * x
        return tuple(total)

    zeros = tuple(jnp.zeros((NTILE, 8, 128), f32) for _ in range(3)) + tuple(jnp.zeros((1, 128), f32) for _ in range(5))
    m0, m1, m2, g0, g1, g2, g3, g4 = lax.fori_loop(0, N, add, zeros)
    c00 = g2 * g4 - g3 * g3
    c01 = g2 * g3 - g1 * g4
    c02 = g1 * g3 - g2 * g2
    c11 = g0 * g4 - g2 * g2
    c12 = g1 * g2 - g0 * g3
    c22 = g0 * g2 - g1 * g1
    det = g0 * c00 + g1 * c01 + g2 * c02
    a0 = ((c00 * m0 + c01 * m1 + c02 * m2) / det).astype(bf16).astype(f32)
    a1 = ((c01 * m0 + c11 * m1 + c12 * m2) / det).astype(bf16).astype(f32)
    a2 = ((c02 * m0 + c12 * m1 + c22 * m2) / det).astype(bf16).astype(f32)
    both = []
    for c in range(2):
        x = channel_at(2 * freq + c)
        both.append(a0 + a1 * x + a2 * (x * x))
    send_b[...] = jnp.stack(both, axis=1).reshape(64, 128).astype(bf16)
    model[facet] = send_b[...]
    start_b()

    land_b()
    copies_m[2].start()
    for t in range(NTILE):
        block = model[:, 16 * t : 16 * t + 16, :].reshape(256, 128)
        half_way = jnp.dot(rows[...], block, preferred_element_type=f32).astype(bf16)
        half_way = jnp.concatenate([half_way[0:64], half_way[64:128]], axis=1)
        tiles[t] = jnp.dot(half_way, cols[...], preferred_element_type=f32)

    lane = lax.broadcasted_iota(jnp.int32, (32, 128), 1)
    re, im = slice(0, FRAME), slice(FRAME, 2 * FRAME)

    def copy_w(c, to, slot):
        return pltpu.make_async_remote_copy(
            src_ref=send_w.at[c, to], dst_ref=out_ref.at[c, slot],
            send_sem=send_sems.at[3 + c, to], recv_sem=recv_sems.at[3 + c, slot],
            device_id={"facet": to}, device_id_type=MESH,
        )

    def facet_row(c, step):
        a = (facet // FCOLS + (N - 1 - step)) % FCOLS
        base = 32 * c
        for t in range(NTILE):
            phase = row_ph[base : base + 32]
            rc = jnp.sum(jnp.where(lane == t * FCOLS + a, phase, 0.0), axis=1, keepdims=True)
            rs = jnp.sum(jnp.where(lane == t * FCOLS + a + 16, phase, 0.0), axis=1, keepdims=True)
            tr, ti = tiles[t, base : base + 32, re], tiles[t, base : base + 32, im]
            shifted[t, :, re] = rc * tr - rs * ti
            shifted[t, :, im] = rc * ti + rs * tr

        for pair in range(2):
            picks = []
            for b in (2 * pair, 2 * pair + 1):
                which = jnp.max(psf_of[a * FCOLS + b].astype(f32))
                picks.append([jnp.where(which == p, 1.0, 0.0) for p in range(4)])

            def product(half, g):
                b = 2 * pair + half
                at = slice(8 * g, 8 * g + 8)
                sr = si = hr = hi = 0.0
                for t in range(NTILE):
                    cc = col_ph[0, t * FCOLS + b : t * FCOLS + b + 1]
                    cs = col_ph[1, t * FCOLS + b : t * FCOLS + b + 1]
                    tr, ti = shifted[t, at, re], shifted[t, at, im]
                    sr = sr + (cc * tr - cs * ti)
                    si = si + (cc * ti + cs * tr)
                for p in range(4):
                    hr = hr + picks[half][p] * psf_sum[c, p, 0, at]
                    hi = hi + picks[half][p] * psf_sum[c, p, 1, at]
                return sr * hr - si * hi, sr * hi + si * hr

            for n in range(3):
                low, high = (product((2 * n + m) // 3, (2 * n + m) % 3) for m in range(2))
                at = slice(48 * pair + 16 * n, 48 * pair + 16 * n + 16)
                prod[at, re] = jnp.concatenate([low[0], high[0]], axis=0).astype(bf16)
                prod[at, im] = jnp.concatenate([low[1], high[1]], axis=0).astype(bf16)

            @pl.when(middle)
            def _():
                for half in range(2):
                    at = slice(48 * pair + 16 * half, 48 * pair + 16 * half + 16)
                    pr, pi = product(half, 0)
                    more_r, more_i = product(half, 3)
                    lead, near = (pr - more_i, pi + more_r), product(0, 1 + half)
                    low, high = (lead, near) if half == 0 else (near, lead)
                    prod[at, re] = jnp.concatenate([low[0], high[0]], axis=0).astype(bf16)
                    prod[at, im] = jnp.concatenate([low[1], high[1]], axis=0).astype(bf16)

        w = jnp.dot(prod[...], back[...], preferred_element_type=f32)
        for b in range(FCOLS):
            part = w[SLOTS * b : SLOTS * (b + 1)]
            both = jnp.concatenate([part[:, 0:FS], part[:, FS : 2 * FS]], axis=0)
            send_w[c, a * FCOLS + b] = both.astype(bf16)
        for n in range(FCOLS):
            to = a * FCOLS + (facet + n) % FCOLS

            @pl.when(to != facet)
            def _():
                copy_w(c, to, facet).start()

    land_f()
    for c in range(2):
        for copy_m in copies_m[c : 2 * c + 1]:
            copy_m.wait()
        for index in range(8):
            if index % 2 == 0:
                values = far[c, 24 * index : 24 * index + 48].astype(f32)
            value = values[24 * (index % 2) : 24 * (index % 2) + 24]
            p, ri = index // 2, index % 2
            sign = 1.0 - 2.0 * ri
            lead = jnp.where(lead_row & upper, 0.0, value[0:8])
            psf_sum[c, p, ri, 0:8] = psf_sum[c, p, ri, 0:8] + sign * lead
            psf_sum[c, p, ri, 8:24] = psf_sum[c, p, ri, 8:24] + sign * value[8:24]

        def row_step(step, _):
            facet_row(c, step)
            return 0

        lax.fori_loop(0, FCOLS, row_step, 0)
        out_ref[c, facet] = send_w[c, facet]
    leave_a()
    leave_f()
    leave_b()

    def land_w(d, _):
        for c in range(2):
            copy_w(c, (facet + N - d) % N, (facet + N - d) % N).wait()
        return 0

    lax.fori_loop(1, N, land_w, 0)


def phases(facet, tile_pos):
    def turn(index, offset):
        index = index * offset
        theta = (index - jnp.floor(index * (1.0 / FRAME)) * FRAME) * (2.0 * math.pi / FRAME)
        counted = jnp.where((offset >= 0.0) & (offset <= FRAME - TS), 1.0, 0.0)
        return jnp.cos(theta) * counted, -jnp.sin(theta) * counted

    def offsets(place, dim):
        tile = place // FCOLS % NTILE
        at = jnp.zeros(place.shape, jnp.int32)
        for t in range(NTILE):
            at = jnp.where(tile == t, tile_pos[dim, t], at)
        return (at - place % FCOLS * FS + PAD).astype(f32)

    row = lax.broadcasted_iota(jnp.int32, (64, 128), 0)
    lane = lax.broadcasted_iota(jnp.int32, (64, 128), 1)
    slot = row % 32
    k = facet * ROWS + jnp.where((slot == 0) & (facet >= N // 2), 0, SLOTS + slot)
    k = jnp.where(slot >= SLOTS, 0, k).astype(f32)
    cos, sin = turn(k, offsets(lane, 0))
    rows = jnp.where(lane < 16, cos, sin)
    place = lax.broadcasted_iota(jnp.int32, (16, FRAME), 0)
    l = lax.broadcasted_iota(jnp.int32, (16, FRAME), 1).astype(f32)
    return rows, jnp.stack(turn(l, offsets(place, 1)))


def convolve(*args):
    dma = pltpu.SemaphoreType.DMA
    return pl.pallas_call(
        convolve_kernel,
        out_shape=jax.ShapeDtypeStruct((2, N, 48, FS), bf16),
        in_specs=[HBM] * 11,
        out_specs=VMEM,
        scratch_shapes=[
            pltpu.VMEM((64, 128), bf16),
            pltpu.SMEM((2,), f32),
            pltpu.SMEM((1,), jnp.int32),
            pltpu.SMEM((2, NTILE), jnp.int32),
            pltpu.VMEM((4, 2, 2, ROWS, FRAME), bf16),
            pltpu.VMEM((48, 96), bf16),
            pltpu.VMEM((48, 96), bf16),
            pltpu.VMEM((128, 256), bf16),
            pltpu.VMEM((256, 2 * FRAME), bf16),
            pltpu.VMEM((FRAME, FRAME), bf16),
            pltpu.VMEM((2 * FRAME, 2 * FS), bf16),
            pltpu.VMEM((80, 128), bf16),
            pltpu.VMEM((N, 80, 128), bf16),
            pltpu.VMEM((64, 128), bf16),
            pltpu.VMEM((N, 64, 128), bf16),
            pltpu.VMEM((16, 128), bf16),
            pltpu.VMEM((N, 16, 128), bf16),
            pltpu.VMEM((16, FRAME), bf16),
            pltpu.VMEM((16, FRAME), bf16),
            pltpu.VMEM((2, 4 * 48, FRAME), bf16),
            pltpu.VMEM((2, 4 * 48, FRAME), bf16),
            pltpu.VMEM((2, 4, 2, 32, FRAME), f32),
            pltpu.VMEM((2, 4 * 48, FRAME), bf16),
            pltpu.VMEM((64, 128), f32),
            pltpu.VMEM((2, 16, FRAME), f32),
            pltpu.VMEM((NTILE, 64, 2 * FRAME), f32),
            pltpu.VMEM((NTILE, 32, 2 * FRAME), f32),
            pltpu.VMEM((FCOLS * SLOTS, 2 * FRAME), bf16),
            pltpu.VMEM((2, N, 48, FS), bf16),
            dma((11,)), dma((5, N)), dma((5, N)), dma((8,)),
        ],
        compiler_params=pltpu.CompilerParams(collective_id=0, has_side_effects=True, vmem_limit_bytes=56 * MIB),
        name="convolve",
    )(*args)


def rows_kernel(residual_ref, w_ref, back_ref, out_ref):
    convolved = jnp.dot(back_ref[...], w_ref[0], preferred_element_type=f32)
    out_ref[0, 0] = residual_ref[0, 0] - convolved * (1.0 / (FRAME * FRAME))


def subtract(residual, w, back):
    return pl.pallas_call(
        rows_kernel,
        grid=(2,),
        out_shape=jax.ShapeDtypeStruct(residual.shape, f32),
        in_specs=[
            pl.BlockSpec((1, 1, FS, FS), lambda c: (c, 0, 0, 0)),
            pl.BlockSpec((1, FRAME, FS), lambda c: (c, 0, 0)),
            pl.BlockSpec((FS, FRAME), lambda c: (0, 0)),
        ],
        out_specs=pl.BlockSpec((1, 1, FS, FS), lambda c: (c, 0, 0, 0)),
        compiler_params=pltpu.CompilerParams(vmem_limit_bytes=24 * MIB),
        name="subtract",
    )(residual, w, back)


def shards(residual, components, chan_weight, tile_pos, facet_psf, psf_spectra):
    table = {name: jnp.asarray(value) for name, value in tables().items()}
    w = convolve(
        components.reshape(64, 128), chan_weight, facet_psf, tile_pos.T, psf_spectra,
        *(table[name] for name in ("mirror", "own", "rows", "cols", "flip", "back_cols")),
    )
    return subtract(residual, w.reshape(2, FRAME, FS), table["back_rows"])


def solution(mesh):
    placed = (
        P("freq", "facet", None, None),
        P(None, "freq", "facet", None),
        P("freq"),
        P(),
        P("facet"),
        P(None, "freq", None, "facet", None),
    )
    return jax.shard_map(
        shards,
        mesh=mesh,
        in_specs=placed,
        out_specs=P("freq", "facet", None, None),
        check_vma=False,
    )
```

```python
import functools
import math

import jax
import jax.numpy as jnp
import ml_dtypes
import numpy as np
from jax import lax
from jax.experimental import pallas as pl
from jax.experimental.pallas import tpu as pltpu
from jax.sharding import PartitionSpec as P

CHAN = 32
FS = 512
PAD = 128
TS = 128
NTILE = 4
FCOLS = 4
FRAME = 768
N = 16
ROWS = 48
AHEAD = 48
SLOTS = 24
MIB = 1 << 20
MESH = pl.DeviceIdType.MESH
VMEM = pl.BlockSpec(memory_space=pltpu.VMEM)
HBM = pl.BlockSpec(memory_space=pltpu.HBM)
f32 = jnp.float32
bf16 = jnp.bfloat16


def own_row(m, slot):
    return 0 if slot == 0 and m >= N // 2 else SLOTS + slot


def angles(left, right):
    return (left * right % FRAME).astype(np.float64) * (2.0 * math.pi / FRAME)


def half(table):
    return table.astype(ml_dtypes.bfloat16)


@functools.cache
def tables():
    chan_of = np.arange(64) // 32
    k_rows = np.zeros((N, 64), np.int64)
    own = np.zeros((N, 48, 96))
    mirror = np.zeros((48, 96))
    for m in range(N):
        for c in range(2):
            for slot in range(SLOTS):
                k_rows[m, 32 * c + slot] = ROWS * m + own_row(m, slot)
                own[m, SLOTS * c + slot, ROWS * c + own_row(m, slot)] = 1.0
    for c in range(2):
        for slot in range(SLOTS):
            mirror[SLOTS * c + slot, ROWS * c + SLOTS - slot] = 1.0
    tile_rows = np.arange(N)[:, None, None] * 8 + np.arange(8)[None, None, :]
    tile_rows = np.broadcast_to(tile_rows, (N, 2, 8)).reshape(-1)
    tile_chan = np.broadcast_to(np.arange(2)[None, :, None], (N, 2, 8)).reshape(-1)
    theta = angles(k_rows[:, :, None], tile_rows[None, None, :])
    same = (chan_of[:, None] == tile_chan[None, :])[None]
    rows = np.concatenate([np.cos(theta) * same, -np.sin(theta) * same], axis=1)
    theta = angles(np.arange(TS)[:, None], np.arange(FRAME)[None, :])
    cos, sin = np.cos(theta), np.sin(theta)
    cols = np.block([[cos, -sin], [sin, cos]])
    theta = angles(np.arange(FRAME)[:, None], PAD + np.arange(FS)[None, :])
    cos, sin = np.cos(theta), np.sin(theta)
    back_cols = np.block([[cos, sin], [-sin, cos]])
    back_rows = np.zeros((FS, N, 2, SLOTS))
    y = PAD + np.arange(FS)
    for m in range(N):
        for slot in range(SLOTS):
            theta = angles(np.int64(ROWS * m + own_row(m, slot)), y)
            back_rows[:, m, 0, slot] = np.cos(theta)
            back_rows[:, m, 1, slot] = -np.sin(theta)
    back_rows[:, N // 2, 0, 0] *= 0.5
    back_rows[:, N // 2, 1, 0] = 0.5
    flip = np.zeros((FRAME, FRAME))
    flip[(FRAME - np.arange(FRAME)) % FRAME, np.arange(FRAME)] = 1.0
    return dict(
        own=half(own),
        mirror=half(mirror),
        rows=half(rows),
        cols=half(cols),
        back_cols=half(back_cols),
        back_rows=half(back_rows.reshape(FS, N * 2 * SLOTS)),
        flip=half(flip),
    )


def channel_at(index):
    return (2 * index - (CHAN - 1)).astype(f32) * (1.0 / CHAN)


def convolve_kernel(
    comps_hbm, weight_hbm, psf_of_hbm, tile_pos_hbm, psf_hbm, mirror_hbm, own_hbm, rows_hbm, cols_hbm, flip_hbm, back_hbm,
    out_ref,
    comps, weight, psf_own, tile_pos, psf, mirror, own, rows, cols, flip, back,
    send_a, recv_a, send_b, model, send_f, psf_of, send_0, far_0, send_m, far,
    psf_sum, turned, row_ph, col_ph, tiles, shifted, prod, send_w,
    local, send_sems, recv_sems, pair_sems,
):
    facet = lax.axis_index("facet")
    freq = lax.axis_index("freq")
    middle = facet == N // 2
    upper = facet >= N // 2
    barrier = pltpu.get_barrier_semaphore()

    def greet(d, _):
        pl.semaphore_signal(barrier, inc=1, device_id={"freq": (freq + d) % N}, device_id_type=MESH)
        pl.semaphore_signal(barrier, inc=1, device_id={"facet": (facet + d) % N}, device_id_type=MESH)
        return 0

    lax.fori_loop(1, N, greet, 0)
    sources = (
        comps_hbm, weight_hbm, psf_of_hbm, psf_hbm, mirror_hbm, flip_hbm,
        own_hbm.at[facet], rows_hbm.at[facet], tile_pos_hbm, cols_hbm, back_hbm,
    )
    targets = (comps, weight, psf_own, psf, mirror, flip, own, rows, tile_pos, cols, back)
    loads = [pltpu.make_async_copy(*pair, local.at[at]) for at, pair in enumerate(zip(sources, targets))]
    for load in loads:
        load.start()

    def copies(at, axis, source, target):
        me = facet if axis == "facet" else freq

        def copy(d, slot):
            return pltpu.make_async_remote_copy(
                src_ref=source, dst_ref=target.at[slot],
                send_sem=send_sems.at[at, d], recv_sem=recv_sems.at[at, slot],
                device_id={axis: (me + d) % N}, device_id_type=MESH,
            )

        def start(d, _):
            copy(d, me).start()
            return 0

        def land(d, _):
            copy(d, (me + N - d) % N).wait_recv()
            return 0

        def leave(d, _):
            copy(d, me).wait_send()
            return 0

        return tuple(functools.partial(lax.fori_loop, 1, N, step, 0) for step in (start, land, leave))

    start_a, land_a, leave_a = copies(0, "freq", send_a, recv_a)
    start_b, land_b, leave_b = copies(1, "facet", send_b, model)
    start_f, land_f, leave_f = copies(2, "facet", send_f, psf_of)

    for load in loads[:3]:
        load.wait()
    send_a[0:64, :] = comps[...]
    row = lax.broadcasted_iota(jnp.int32, (8, 128), 0)
    parts = []
    for c in range(2):
        whole = jnp.full((8, 128), weight[c], f32)
        first = whole.astype(bf16).astype(f32)
        second = (whole - first).astype(bf16).astype(f32)
        third = (whole - first) - second
        parts.append(jnp.where(row == 0, first, jnp.where(row == 1, second, jnp.where(row == 2, third, 0.0))))
    send_a[64:80, :] = jnp.concatenate(parts, axis=0).astype(bf16)
    send_f[...] = jnp.full((16, 128), psf_own[0].astype(f32), f32).astype(bf16)
    recv_a[freq] = send_a[...]
    psf_of[facet] = send_f[...]

    loads[3].wait()
    loads[4].wait()
    loads[5].wait()
    for p in range(4):
        parts = [
            jnp.dot(mirror[...], psf[p, :, ri].reshape(2 * ROWS, FRAME), preferred_element_type=f32) for ri in range(2)
        ]
        for c in range(2):
            part = jnp.concatenate([part[SLOTS * c : SLOTS * (c + 1)] for part in parts], axis=0)
            turned[c, 48 * p : 48 * (p + 1)] = part.astype(bf16)
    send_m[...] = (
        jnp.dot(turned[...].reshape(8 * 48, FRAME), flip[...], preferred_element_type=f32)
        .astype(bf16)
        .reshape(2, 4 * 48, FRAME)
    )
    send_0[...] = jnp.concatenate(
        [psf[n // 4, n // 2 % 2, n % 2, 0:1].astype(f32) for n in range(16)], axis=0
    ).astype(bf16)
    copies_m = [
        pltpu.make_async_remote_copy(
            src_ref=send_m.at[c, part], dst_ref=far.at[c, part],
            send_sem=pair_sems.at[2 + at], recv_sem=pair_sems.at[5 + at],
            device_id={"facet": N - 1 - facet}, device_id_type=MESH,
        )
        for at, (c, part) in enumerate(
            ((0, pl.ds(0, 192)), (1, pl.ds(0, AHEAD)), (1, pl.ds(AHEAD, 192 - AHEAD)))
        )
    ]
    is_first = 1 - (facet + N - 1) // N
    is_middle = 1 - ((facet + N // 2) % N + N - 1) // N
    copy_0 = pltpu.make_async_remote_copy(
        src_ref=send_0, dst_ref=far_0, send_sem=pair_sems.at[0], recv_sem=pair_sems.at[1],
        device_id={"facet": (N - facet) % N + (N // 2) * (is_first - is_middle)}, device_id_type=MESH,
    )
    pl.semaphore_wait(barrier, 2 * (N - 1))
    copies_m[0].start()
    start_a()
    copy_0.start()
    copies_m[1].start()
    start_f()

    for load in loads[6:]:
        load.wait()
    for index in range(8):
        both = psf[index // 2, :, index % 2].reshape(2 * ROWS, FRAME)
        chosen = jnp.dot(own[...], both, preferred_element_type=f32)
        for c in range(2):
            psf_sum[c, index // 2, index % 2, 0:SLOTS] = chosen[SLOTS * c : SLOTS * (c + 1)]
    row_ph[...], col_ph[...] = phases(facet, tile_pos)

    copy_0.wait()
    lead_row = lax.broadcasted_iota(jnp.int32, (8, FRAME), 0) == 0
    zeros_there = far_0[...].astype(f32)
    ends = jnp.dot(jnp.concatenate([far_0[...], send_0[...]], axis=0), flip[...], preferred_element_type=f32)
    for n in range(16):
        p, c, ri = n // 4, n // 2 % 2, n % 2
        sign = 1.0 - 2.0 * ri
        there, here = ends[n : n + 1], ends[16 + n : 17 + n]
        psf_sum[c, p, ri, 24:32] = jnp.where(lead_row, zeros_there[n : n + 1] + sign * there, 0.0)
        lead = jnp.where(lead_row & upper, jnp.where(middle, here, there), 0.0)
        psf_sum[c, p, ri, 0:8] = psf_sum[c, p, ri, 0:8] + sign * lead

    land_a()

    def add(q, total):
        total = list(total)
        block = recv_a[q].astype(f32)
        comp = block[0:64].reshape(NTILE, 2, 8, 128)
        for c in range(2):
            x = channel_at(2 * q + c)
            power = jnp.sum(block[64 + 8 * c : 72 + 8 * c], axis=0, keepdims=True)
            for n in range(5):
                if n < 3:
                    total[n] = total[n] + power * comp[:, c]
                total[3 + n] = total[3 + n] + power
                power = power * x
        return tuple(total)

    zeros = tuple(jnp.zeros((NTILE, 8, 128), f32) for _ in range(3)) + tuple(jnp.zeros((1, 128), f32) for _ in range(5))
    m0, m1, m2, g0, g1, g2, g3, g4 = lax.fori_loop(0, N, add, zeros)
    c00 = g2 * g4 - g3 * g3
    c01 = g2 * g3 - g1 * g4
    c02 = g1 * g3 - g2 * g2
    c11 = g0 * g4 - g2 * g2
    c12 = g1 * g2 - g0 * g3
    c22 = g0 * g2 - g1 * g1
    det = g0 * c00 + g1 * c01 + g2 * c02
    a0 = ((c00 * m0 + c01 * m1 + c02 * m2) / det).astype(bf16).astype(f32)
    a1 = ((c01 * m0 + c11 * m1 + c12 * m2) / det).astype(bf16).astype(f32)
    a2 = ((c02 * m0 + c12 * m1 + c22 * m2) / det).astype(bf16).astype(f32)
    both = []
    for c in range(2):
        x = channel_at(2 * freq + c)
        both.append(a0 + a1 * x + a2 * (x * x))
    send_b[...] = jnp.stack(both, axis=1).reshape(64, 128).astype(bf16)
    model[facet] = send_b[...]
    start_b()

    def add_mirror(c):
        for copy_m in copies_m[c : 2 * c + 1]:
            copy_m.wait()
        for index in range(8):
            if index % 2 == 0:
                values = far[c, 24 * index : 24 * index + 48].astype(f32)
            value = values[24 * (index % 2) : 24 * (index % 2) + 24]
            p, ri = index // 2, index % 2
            sign = 1.0 - 2.0 * ri
            lead = jnp.where(lead_row & upper, 0.0, value[0:8])
            psf_sum[c, p, ri, 0:8] = psf_sum[c, p, ri, 0:8] + sign * lead
            psf_sum[c, p, ri, 8:24] = psf_sum[c, p, ri, 8:24] + sign * value[8:24]

    land_f()
    add_mirror(0)

    land_b()
    copies_m[2].start()
    for t in range(NTILE):
        block = model[:, 16 * t : 16 * t + 16, :].reshape(256, 128)
        half_way = jnp.dot(rows[...], block, preferred_element_type=f32).astype(bf16)
        half_way = jnp.concatenate([half_way[0:64], half_way[64:128]], axis=1)
        tiles[t] = jnp.dot(half_way, cols[...], preferred_element_type=f32)

    lane = lax.broadcasted_iota(jnp.int32, (32, 128), 1)
    re, im = slice(0, FRAME), slice(FRAME, 2 * FRAME)

    def copy_w(c, to, slot):
        return pltpu.make_async_remote_copy(
            src_ref=send_w.at[c, to], dst_ref=out_ref.at[c, slot],
            send_sem=send_sems.at[3 + c, to], recv_sem=recv_sems.at[3 + c, slot],
            device_id={"facet": to}, device_id_type=MESH,
        )

    def facet_row(c, step):
        a = (facet // FCOLS + (N - 1 - step)) % FCOLS
        base = 32 * c
        for t in range(NTILE):
            phase = row_ph[base : base + 32]
            rc = jnp.sum(jnp.where(lane == t * FCOLS + a, phase, 0.0), axis=1, keepdims=True)
            rs = jnp.sum(jnp.where(lane == t * FCOLS + a + 16, phase, 0.0), axis=1, keepdims=True)
            tr, ti = tiles[t, base : base + 32, re], tiles[t, base : base + 32, im]
            shifted[t, :, re] = rc * tr - rs * ti
            shifted[t, :, im] = rc * ti + rs * tr

        for pair in range(2):
            picks = []
            for b in (2 * pair, 2 * pair + 1):
                which = jnp.max(psf_of[a * FCOLS + b].astype(f32))
                picks.append([jnp.where(which == p, 1.0, 0.0) for p in range(4)])

            def product(half, g):
                b = 2 * pair + half
                at = slice(8 * g, 8 * g + 8)
                sr = si = hr = hi = 0.0
                for t in range(NTILE):
                    cc = col_ph[0, t * FCOLS + b : t * FCOLS + b + 1]
                    cs = col_ph[1, t * FCOLS + b : t * FCOLS + b + 1]
                    tr, ti = shifted[t, at, re], shifted[t, at, im]
                    sr = sr + (cc * tr - cs * ti)
                    si = si + (cc * ti + cs * tr)
                for p in range(4):
                    hr = hr + picks[half][p] * psf_sum[c, p, 0, at]
                    hi = hi + picks[half][p] * psf_sum[c, p, 1, at]
                return sr * hr - si * hi, sr * hi + si * hr

            for n in range(3):
                low, high = (product((2 * n + m) // 3, (2 * n + m) % 3) for m in range(2))
                at = slice(48 * pair + 16 * n, 48 * pair + 16 * n + 16)
                prod[at, re] = jnp.concatenate([low[0], high[0]], axis=0).astype(bf16)
                prod[at, im] = jnp.concatenate([low[1], high[1]], axis=0).astype(bf16)

            @pl.when(middle)
            def _():
                for half in range(2):
                    at = slice(48 * pair + 16 * half, 48 * pair + 16 * half + 16)
                    pr, pi = product(half, 0)
                    more_r, more_i = product(half, 3)
                    lead, near = (pr - more_i, pi + more_r), product(0, 1 + half)
                    low, high = (lead, near) if half == 0 else (near, lead)
                    prod[at, re] = jnp.concatenate([low[0], high[0]], axis=0).astype(bf16)
                    prod[at, im] = jnp.concatenate([low[1], high[1]], axis=0).astype(bf16)

        w = jnp.dot(prod[...], back[...], preferred_element_type=f32)
        for b in range(FCOLS):
            part = w[SLOTS * b : SLOTS * (b + 1)]
            both = jnp.concatenate([part[:, 0:FS], part[:, FS : 2 * FS]], axis=0)
            send_w[c, a * FCOLS + b] = both.astype(bf16)
        for n in range(FCOLS):
            to = a * FCOLS + (facet + n) % FCOLS

            @pl.when(to != facet)
            def _():
                copy_w(c, to, facet).start()

    for c in range(2):
        if c > 0:
            add_mirror(c)

        def row_step(step, _):
            facet_row(c, step)
            return 0

        lax.fori_loop(0, FCOLS, row_step, 0)
        out_ref[c, facet] = send_w[c, facet]
    leave_a()
    leave_f()
    leave_b()

    def land_w(d, _):
        for c in range(2):
            copy_w(c, (facet + N - d) % N, (facet + N - d) % N).wait()
        return 0

    lax.fori_loop(1, N, land_w, 0)


def phases(facet, tile_pos):
    def turn(index, offset):
        index = index * offset
        theta = (index - jnp.floor(index * (1.0 / FRAME)) * FRAME) * (2.0 * math.pi / FRAME)
        counted = jnp.where((offset >= 0.0) & (offset <= FRAME - TS), 1.0, 0.0)
        return jnp.cos(theta) * counted, -jnp.sin(theta) * counted

    def offsets(place, dim):
        tile = place // FCOLS % NTILE
        at = jnp.zeros(place.shape, jnp.int32)
        for t in range(NTILE):
            at = jnp.where(tile == t, tile_pos[dim, t], at)
        return (at - place % FCOLS * FS + PAD).astype(f32)

    row = lax.broadcasted_iota(jnp.int32, (64, 128), 0)
    lane = lax.broadcasted_iota(jnp.int32, (64, 128), 1)
    slot = row % 32
    k = facet * ROWS + jnp.where((slot == 0) & (facet >= N // 2), 0, SLOTS + slot)
    k = jnp.where(slot >= SLOTS, 0, k).astype(f32)
    cos, sin = turn(k, offsets(lane, 0))
    rows = jnp.where(lane < 16, cos, sin)
    place = lax.broadcasted_iota(jnp.int32, (16, FRAME), 0)
    l = lax.broadcasted_iota(jnp.int32, (16, FRAME), 1).astype(f32)
    return rows, jnp.stack(turn(l, offsets(place, 1)))


def convolve(*args):
    dma = pltpu.SemaphoreType.DMA
    return pl.pallas_call(
        convolve_kernel,
        out_shape=jax.ShapeDtypeStruct((2, N, 48, FS), bf16),
        in_specs=[HBM] * 11,
        out_specs=VMEM,
        scratch_shapes=[
            pltpu.VMEM((64, 128), bf16),
            pltpu.SMEM((2,), f32),
            pltpu.SMEM((1,), jnp.int32),
            pltpu.SMEM((2, NTILE), jnp.int32),
            pltpu.VMEM((4, 2, 2, ROWS, FRAME), bf16),
            pltpu.VMEM((48, 96), bf16),
            pltpu.VMEM((48, 96), bf16),
            pltpu.VMEM((128, 256), bf16),
            pltpu.VMEM((256, 2 * FRAME), bf16),
            pltpu.VMEM((FRAME, FRAME), bf16),
            pltpu.VMEM((2 * FRAME, 2 * FS), bf16),
            pltpu.VMEM((80, 128), bf16),
            pltpu.VMEM((N, 80, 128), bf16),
            pltpu.VMEM((64, 128), bf16),
            pltpu.VMEM((N, 64, 128), bf16),
            pltpu.VMEM((16, 128), bf16),
            pltpu.VMEM((N, 16, 128), bf16),
            pltpu.VMEM((16, FRAME), bf16),
            pltpu.VMEM((16, FRAME), bf16),
            pltpu.VMEM((2, 4 * 48, FRAME), bf16),
            pltpu.VMEM((2, 4 * 48, FRAME), bf16),
            pltpu.VMEM((2, 4, 2, 32, FRAME), f32),
            pltpu.VMEM((2, 4 * 48, FRAME), bf16),
            pltpu.VMEM((64, 128), f32),
            pltpu.VMEM((2, 16, FRAME), f32),
            pltpu.VMEM((NTILE, 64, 2 * FRAME), f32),
            pltpu.VMEM((NTILE, 32, 2 * FRAME), f32),
            pltpu.VMEM((FCOLS * SLOTS, 2 * FRAME), bf16),
            pltpu.VMEM((2, N, 48, FS), bf16),
            dma((11,)), dma((5, N)), dma((5, N)), dma((8,)),
        ],
        compiler_params=pltpu.CompilerParams(collective_id=0, has_side_effects=True, vmem_limit_bytes=56 * MIB),
        name="convolve",
    )(*args)


def rows_kernel(residual_ref, w_ref, back_ref, out_ref):
    convolved = jnp.dot(back_ref[...], w_ref[0], preferred_element_type=f32)
    out_ref[0, 0] = residual_ref[0, 0] - convolved * (1.0 / (FRAME * FRAME))


def subtract(residual, w, back):
    return pl.pallas_call(
        rows_kernel,
        grid=(2,),
        out_shape=jax.ShapeDtypeStruct(residual.shape, f32),
        in_specs=[
            pl.BlockSpec((1, 1, FS, FS), lambda c: (c, 0, 0, 0)),
            pl.BlockSpec((1, FRAME, FS), lambda c: (c, 0, 0)),
            pl.BlockSpec((FS, FRAME), lambda c: (0, 0)),
        ],
        out_specs=pl.BlockSpec((1, 1, FS, FS), lambda c: (c, 0, 0, 0)),
        compiler_params=pltpu.CompilerParams(vmem_limit_bytes=24 * MIB),
        name="subtract",
    )(residual, w, back)


def shards(residual, components, chan_weight, tile_pos, facet_psf, psf_spectra):
    table = {name: jnp.asarray(value) for name, value in tables().items()}
    w = convolve(
        components.reshape(64, 128), chan_weight, facet_psf, tile_pos.T, psf_spectra,
        *(table[name] for name in ("mirror", "own", "rows", "cols", "flip", "back_cols")),
    )
    return subtract(residual, w.reshape(2, FRAME, FS), table["back_rows"])


def solution(mesh):
    placed = (
        P("freq", "facet", None, None),
        P(None, "freq", "facet", None),
        P("freq"),
        P(),
        P("facet"),
        P(None, "freq", None, "facet", None),
    )
    return jax.shard_map(
        shards,
        mesh=mesh,
        in_specs=placed,
        out_specs=P("freq", "facet", None, None),
        check_vma=False,
    )
```
